32 devices in a mesh: blk: 8 (over z, y), grp: 4 (over x, core).
Axes of the slice: x: 2, y: 2, z: 4, core: 2. Of those that a mesh axis runs over, the one named last changes fastest.
Arguments:
- queries: bfloat16 [4096, 4096], P(('blk', 'grp')), may hold values from -0.1875 to 0.1875
- passages: bfloat16 [64, 4096], P(('blk', 'grp')), may hold values from -5 to 5
- pool: bfloat16 [4096, 4096], P(('blk', 'grp')), may hold values from -5 to 5
- positive_ids: int32 [4096], P(('blk', 'grp')), may hold values from 0 to 15
- request_lists: int32 [32, 4, 32], P(('blk', 'grp')), may hold values from 0 to 127, as said below
- hard_refs: int32 [4096, 30], P(('blk', 'grp')), may hold values from 0 to 127, as said below
- hard_count: int32 [4096], P(('blk', 'grp')), may hold values from 1 to 30
Outputs:
- query_grad: bfloat16 [4096, 4096], P(('blk', 'grp'))
- query_loss: float32 [4096], P(('blk', 'grp'))
The draws below stay inside these ranges and needn't reach their ends.
Inputs may be any that keep to these rules, and one draw needn't show every extreme that they name: `request_lists`: entries of one list are distinct rows of that owner's 128 pool rows. `hard_refs`: the first hard_count entries of a row are distinct; later entries are padding and unused.
All inputs are finite; a program needn't handle non-finite values.
Results may differ from the reference program's by a relative error of at most 0.0034.
Values may be sent and summed in bfloat16 or wider, within the bound.
A program may use at most 64 MiB of HBM per device.

```python
import math
import jax
import jax.numpy as jnp
from jax import lax

D = 4096
Q_DEV = 128
P_DEV = 2
POOL = 128
SLOTS = 32
HN_MAX = 30
QTOT = 4096
NPAS = 64
NPOOL = 4096
N_BLK = 8
N_GRP = 4


def passage_base(key):
    base = jnp.clip(jax.random.normal(key, (NPAS, D), jnp.float32), -5.0, 5.0)
    base = base.at[0, 0].set(5.0)
    return base.at[1, 1].set(-5.0)


def draw_passages(key, part):
    shared = passage_base(key)
    return shared.astype(jnp.bfloat16)


def draw_queries(key, part):
    key = jax.random.fold_in(key, 11)
    spread = 3.0 / math.sqrt(D)
    base = jnp.clip(jax.random.normal(key, (QTOT, D), jnp.float32), -5.0, 5.0) * spread
    base = jnp.clip(base, -4.0 * spread, 4.0 * spread)
    base = base.at[0, 0].set(4.0 * spread)
    base = base.at[1, 0].set(-4.0 * spread)
    return base.astype(jnp.bfloat16)


def draw_request_lists(key, part):
    key = jax.random.fold_in(key, 37)
    list_keys = jax.random.split(key, N_BLK * N_GRP * N_GRP)
    lists = jax.vmap(lambda list_key: jax.random.permutation(list_key, POOL)[:SLOTS])(list_keys)
    return lists.reshape(N_BLK * N_GRP, N_GRP, SLOTS).astype(jnp.int32)


def draw_hard_refs(key, part):
    key = jax.random.fold_in(key, 23)
    row_keys = jax.random.split(key, QTOT)
    refs = jax.vmap(lambda row_key: jax.random.permutation(row_key, N_GRP * SLOTS)[:HN_MAX])(row_keys)
    return refs.astype(jnp.int32)


def draw_hard_count(key, part):
    key = jax.random.fold_in(key, 29)
    key_a, key_b, key_c = jax.random.split(key, 3)
    counts = jax.random.randint(key_a, (QTOT,), 1, HN_MAX + 1, jnp.int32)
    full_row = jax.random.randint(key_b, (), 0, QTOT, jnp.int32)
    short_row = (full_row + 1 + jax.random.randint(key_c, (), 0, QTOT - 1, jnp.int32)) % QTOT
    counts = counts.at[full_row].set(HN_MAX)
    counts = counts.at[short_row].set(1)
    return counts.astype(jnp.int32)


def touch_ends(values, stream_key, smallest, top_value):
    longest = values.shape.index(max(values.shape))
    spots = []
    for shift in (0, 1):
        where = [jax.random.randint(jax.random.fold_in(stream_key, axis), (), 0, length) for axis, length in enumerate(values.shape)]
        where[longest] = (where[longest] + shift) % values.shape[longest]
        spots.append(tuple(where))
    return values.at[spots[0]].set(smallest).at[spots[1]].set(top_value)


def block_scale(rng, dims, cuts, low, largest):
    factor_of, own = 1.0, jax.random.fold_in(rng, 6)
    for axis_at, blocks in cuts:
        steps = jnp.exp(jax.random.uniform(jax.random.fold_in(own, axis_at), (blocks,), jnp.float32, low / len(cuts), largest / len(cuts)))
        factor_of = factor_of * jnp.repeat(steps, dims[axis_at] // blocks).reshape([-1 if axis == axis_at else 1 for axis in range(len(dims))])
    return factor_of


def noise(key, shape, width, reach, pieces=(), kind=jnp.bfloat16):
    factor_of = block_scale(key, shape, pieces, -0.22, 0.18) if pieces else 1.0
    entries = jax.random.normal(key, shape, jnp.float32) * width * factor_of
    return jnp.minimum(jnp.maximum(entries, -reach), reach).astype(kind)


def setup_inputs(seed: int = 0) -> dict:
    arg_keys = jax.random.split(jax.random.key(seed), 8)
    queries = draw_queries(jax.random.fold_in(arg_keys[7], 71), 0)
    passages = draw_passages(jax.random.fold_in(arg_keys[7], 71), 0)
    pool = noise(arg_keys[2], (NPOOL, D), 1.0, 5.0, ((0, 32),))
    positive_ids = touch_ends(jax.random.randint(arg_keys[3], (QTOT,), 0, P_DEV * N_BLK), jax.random.fold_in(arg_keys[3], 1), 0, (P_DEV * N_BLK) - 1).astype(jnp.int32)
    request_lists = draw_request_lists(jax.random.fold_in(arg_keys[7], 71), 0)
    hard_refs = draw_hard_refs(jax.random.fold_in(arg_keys[7], 71), 0)
    hard_count = draw_hard_count(jax.random.fold_in(arg_keys[7], 71), 0)
    return {"queries": queries, "passages": passages, "pool": pool, "positive_ids": positive_ids, "request_lists": request_lists, "hard_refs": hard_refs, "hard_count": hard_count}


def hard_mask(refs, count, span):
    table_iota = jnp.arange(span, dtype=jnp.int32)
    order = jnp.arange(refs.shape[1], dtype=jnp.int32)
    live = order[None, :] < count[:, None]
    hits = (refs[:, :, None] == table_iota[None, None, :]) & live[:, :, None]
    return jnp.sum(hits.astype(jnp.float32), axis=1)


def contrast(query_rows, cycle_rows, hard_table, positive, present):
    cycle_logits = jnp.dot(query_rows, cycle_rows.T, preferred_element_type=jnp.float32)
    hard_logits = jnp.dot(query_rows, hard_table.T, preferred_element_type=jnp.float32)
    hard_peak = jnp.max(jnp.where(present > 0, hard_logits, -jnp.inf), axis=1)
    peak_value = jnp.maximum(hard_peak, jnp.max(cycle_logits, axis=1))
    cycle_exp = jnp.exp(cycle_logits - peak_value[:, None])
    hard_exp = present * jnp.exp(hard_logits - peak_value[:, None])
    denominator = jnp.sum(cycle_exp, axis=1) + jnp.sum(hard_exp, axis=1)
    cycle_iota = jnp.arange(cycle_rows.shape[0], dtype=jnp.int32)
    onehot = (cycle_iota[None, :] == positive[:, None]).astype(jnp.float32)
    chosen = jnp.sum(cycle_logits * onehot, axis=1)
    query_loss = jnp.log(denominator) + peak_value - chosen
    cycle_weights = (cycle_exp / denominator[:, None] - onehot).astype(jnp.bfloat16)
    hard_weights = (hard_exp / denominator[:, None]).astype(jnp.bfloat16)
    summed = jnp.dot(cycle_weights, cycle_rows, preferred_element_type=jnp.float32)
    summed = summed + jnp.dot(hard_weights, hard_table, preferred_element_type=jnp.float32)
    return summed.astype(jnp.bfloat16), query_loss


def reference(queries, passages, pool, positive_ids, request_lists, hard_refs, hard_count):
    passage_grid = passages.reshape(N_BLK, N_GRP, P_DEV, D)
    pool_grid = pool.reshape(N_BLK, N_GRP, POOL, D)

    def device_work(device):
        blk_index = device // N_GRP
        grp_index = device % N_GRP
        cycle_rows = lax.dynamic_index_in_dim(passage_grid, grp_index, 1, keepdims=False).reshape(N_BLK * P_DEV, D)
        owner_pool = lax.dynamic_index_in_dim(pool_grid, blk_index, 0, keepdims=False)
        lists_here = lax.dynamic_index_in_dim(request_lists, device, 0, keepdims=False)
        hard_table = jax.vmap(lambda rows_of, picked_rows: rows_of[picked_rows])(owner_pool, lists_here)
        hard_table = hard_table.reshape(N_GRP * SLOTS, D)
        first_row = (device * Q_DEV).astype(jnp.int32)
        query_rows = lax.dynamic_slice_in_dim(queries, first_row, Q_DEV, 0)
        positive = lax.dynamic_slice_in_dim(positive_ids, first_row, Q_DEV, 0)
        refs_here = lax.dynamic_slice_in_dim(hard_refs, first_row, Q_DEV, 0)
        count_here = lax.dynamic_slice_in_dim(hard_count, first_row, Q_DEV, 0)
        present = hard_mask(refs_here, count_here, N_GRP * SLOTS)
        return contrast(query_rows, cycle_rows, hard_table, positive, present)

    grads, losses = lax.map(device_work, jnp.arange(N_BLK * N_GRP, dtype=jnp.int32))
    return grads.reshape(QTOT, D), losses.reshape(QTOT)
```

```python
import functools

import jax
import jax.numpy as jnp
from jax import lax
from jax.experimental import pallas as pl
from jax.experimental.pallas import tpu as pltpu
from jax.sharding import PartitionSpec as P

MESH = pl.DeviceIdType.MESH
CHUNKS = 4
GRAD_TILES = 4
VMEM_LIMIT = 32 * 2**20
TILE_ROWS = 16


def iota(shape, axis):
    return lax.broadcasted_iota(jnp.int32, shape, axis)


def dot_nt(a, b):
    return lax.dot_general(a, b, (((1,), (1,)), ((), ())), preferred_element_type=jnp.float32)


def dot_nn(a, b):
    return jnp.dot(a, b, preferred_element_type=jnp.float32)


def kernel(n_blk, queries, passages, pool, positive, lists, refs, count, table, weights, loss,
           q_v, pass_v, pool_v, pos_v, list_v, refs_v, count_v,
           hot_out, hot_in, picked, packed,
           load_sem, hot_send, hot_recv, row_send, row_recv, pass_send, pass_recv):
    blk = lax.axis_index("blk")
    grp = lax.axis_index("grp")
    q_rows, depth = q_v.shape
    p_dev = pass_v.shape[0]
    pool_rows = pool_v.shape[0]
    owners, slots = list_v.shape
    span = owners * slots
    cycle = n_blk * p_dev
    folds = TILE_ROWS // p_dev
    fold_w = depth // folds
    width = depth // CHUNKS

    half, core = lax.div(grp, 2), lax.rem(grp, 2)
    far, side = 1 - half, 1 - core
    peers = {1: half * 2 + side, 2: far * 2 + core, 3: far * 2 + side}

    barrier = pltpu.get_barrier_semaphore()
    for step in (1, 2, 3):
        pl.semaphore_signal(barrier, inc=1, device_id={"grp": peers[step]}, device_id_type=MESH)

    def greet(step, carry):
        pl.semaphore_signal(barrier, inc=1, device_id={"blk": lax.rem(blk + step, n_blk)}, device_id_type=MESH)
        return carry

    lax.fori_loop(1, n_blk, greet, 0)

    loads = [
        pltpu.make_async_copy(src, dst, load_sem.at[i])
        for i, (src, dst) in enumerate((
            (lists, list_v), (passages, pass_v), (pool, pool_v), (refs, refs_v),
            (count, count_v), (positive, pos_v), (queries, q_v)))
    ]
    for load in loads:
        load.start()

    loads[0].wait()
    eye = iota((slots, slots), 0) == iota((slots, slots), 1)
    pool_iota = iota((slots, pool_rows), 1).astype(jnp.float32)
    wanted = list_v[...].astype(jnp.float32)
    for o in range(owners):
        column = jnp.sum(jnp.where(eye, wanted[o:o + 1, :], 0.0), axis=1, keepdims=True)
        hot_out[o * slots:(o + 1) * slots, :] = (pool_iota == column).astype(jnp.float32).astype(jnp.bfloat16)

    loads[1].wait()
    own = pass_v[...].astype(jnp.float32)
    fold_iota = iota((TILE_ROWS, fold_w), 0)
    folded = jnp.zeros((TILE_ROWS, fold_w), jnp.float32)
    for c in range(folds):
        for j in range(p_dev):
            folded = jnp.where(fold_iota == c * p_dev + j, own[j:j + 1, c * fold_w:(c + 1) * fold_w], folded)
    own_slot = pl.ds(pl.multiple_of(blk * TILE_ROWS, TILE_ROWS), TILE_ROWS)
    packed[own_slot, :] = folded.astype(jnp.bfloat16)

    pl.semaphore_wait(barrier, owners - 1 + n_blk - 1)

    hot_copies = {}
    for step in (2, 3, 1):
        hot_copies[step] = pltpu.make_async_remote_copy(
            src_ref=hot_out.at[pl.ds(pl.multiple_of(peers[step] * slots, slots), slots)],
            dst_ref=hot_in.at[pl.ds(step * slots, slots)],
            send_sem=hot_send.at[step], recv_sem=hot_recv.at[step],
            device_id={"grp": peers[step]}, device_id_type=MESH)
        hot_copies[step].start()

    def pass_copy(step):
        return pltpu.make_async_remote_copy(
            src_ref=packed.at[own_slot], dst_ref=packed.at[own_slot],
            send_sem=pass_send.at[step], recv_sem=pass_recv.at[step],
            device_id={"blk": lax.rem(blk + step, n_blk)}, device_id_type=MESH)

    def send_pass(step, carry):
        pass_copy(step).start()
        return carry

    lax.fori_loop(1, n_blk, send_pass, 0)

    own_rows = pl.ds(pl.multiple_of(grp * slots, slots), slots)
    hot_in[0:slots, :] = hot_out[own_rows, :]
    loads[2].wait()
    for step in (1, 2, 3):
        hot_copies[step].wait_recv()
    row_copies = []
    for c in range(CHUNKS):
        cols = slice(c * width, (c + 1) * width)
        rows = dot_nn(hot_in[...], pool_v[:, cols]).astype(jnp.bfloat16)
        picked[:, cols] = rows
        table[own_rows, cols] = rows[0:slots, :]
        sent = {}
        for step in (2, 3, 1):
            sent[step] = pltpu.make_async_remote_copy(
                src_ref=picked.at[pl.ds(step * slots, slots), pl.ds(c * width, width)],
                dst_ref=table.at[own_rows, pl.ds(c * width, width)],
                send_sem=row_send.at[step, c], recv_sem=row_recv.at[step, c],
                device_id={"grp": peers[step]}, device_id_type=MESH)
            sent[step].start()
        row_copies.append(sent)

    for load in loads[3:]:
        load.wait()
    hn = refs_v.shape[0]
    refs_t = jnp.where(iota((hn, q_rows), 0) < count_v[...], refs_v[...], -1)
    row_iota = iota((span, q_rows), 0)
    present = jnp.zeros((span, q_rows), jnp.float32)
    for i in range(hn):
        present = present + (row_iota == refs_t[i:i + 1, :]).astype(jnp.float32)

    def recv_pass(step, carry):
        pass_copy(step).wait()
        return carry

    lax.fori_loop(1, n_blk, recv_pass, 0)
    group_rows = folds * TILE_ROWS
    out_row, in_row = iota((group_rows, group_rows), 0), iota((group_rows, group_rows), 1)
    k = lax.rem(out_row, TILE_ROWS)
    source = lax.div(k, p_dev) * TILE_ROWS + lax.div(out_row, TILE_ROWS) * p_dev + lax.rem(k, p_dev)
    unfold = (source == in_row).astype(jnp.float32).astype(jnp.bfloat16)

    def unfold_group(i, carry):
        block = packed[pl.ds(pl.multiple_of(i * group_rows, group_rows), group_rows), :]
        rows = dot_nn(unfold, block).astype(jnp.bfloat16)
        place = pl.ds(pl.multiple_of(span + i * TILE_ROWS, TILE_ROWS), TILE_ROWS)
        for c in range(folds):
            table[place, c * fold_w:(c + 1) * fold_w] = rows[c * TILE_ROWS:(c + 1) * TILE_ROWS, :]
        return carry

    lax.fori_loop(0, n_blk // folds, unfold_group, 0)
    cycle_logits = jnp.zeros((cycle, q_rows), jnp.float32)
    for c in range(CHUNKS):
        cols = slice(c * width, (c + 1) * width)
        cycle_logits = cycle_logits + dot_nt(table[span:span + cycle, cols], q_v[:, cols])
    cycle_peak = jnp.max(cycle_logits, axis=0, keepdims=True)
    onehot = (iota((cycle, q_rows), 0) == pos_v[...]).astype(jnp.float32)
    chosen = jnp.sum(cycle_logits * onehot, axis=0, keepdims=True)

    hard_logits = jnp.zeros((span, q_rows), jnp.float32)
    for c in range(CHUNKS):
        cols = slice(c * width, (c + 1) * width)
        for step in (1, 2, 3):
            row_copies[c][step].wait_recv()
        hard_logits = hard_logits + dot_nt(table[0:span, cols], q_v[:, cols])

    used = present > 0
    masked = jnp.where(used, hard_logits, -jnp.inf)
    peak = jnp.maximum(cycle_peak, jnp.max(masked, axis=0, keepdims=True))
    cycle_exp = jnp.exp(cycle_logits - peak)
    hard_exp = present * jnp.exp(jnp.where(used, hard_logits - peak, 0.0))
    denominator = jnp.sum(cycle_exp, axis=0, keepdims=True) + jnp.sum(hard_exp, axis=0, keepdims=True)
    loss[...] = jnp.log(denominator) + peak - chosen
    scale = 1.0 / denominator
    weights[:, 0:span] = (hard_exp * scale).T.astype(jnp.bfloat16)
    weights[:, span:span + cycle] = (cycle_exp * scale - onehot).T.astype(jnp.bfloat16)

    for step in (1, 2, 3):
        hot_copies[step].wait_send()
        for c in range(CHUNKS):
            row_copies[c][step].wait_send()


def grad_kernel(table, weights, loss, grad, loss_out, grad_v, sems):
    tiles = sems.shape[0] - 1
    width = grad_v.shape[1] // tiles
    copies = [pltpu.make_async_copy(loss, loss_out, sems.at[tiles])]
    copies[0].start()
    for c in range(tiles):
        cols = slice(c * width, (c + 1) * width)
        grad_v[:, cols] = dot_nn(weights[...], table[:, cols]).astype(jnp.bfloat16)
        here = pl.ds(c * width, width)
        copies.append(pltpu.make_async_copy(grad_v.at[:, here], grad.at[:, here], sems.at[c]))
        copies[-1].start()
    for copy in copies:
        copy.wait()


def body(n_blk, queries, passages, pool, positive_ids, request_lists, hard_refs, hard_count):
    q_rows, depth = queries.shape
    p_dev = passages.shape[0]
    pool_rows = pool.shape[0]
    _, owners, slots = request_lists.shape
    hn = hard_refs.shape[1]
    span, cycle = owners * slots, n_blk * p_dev
    bf16, f32, i32 = jnp.bfloat16, jnp.float32, jnp.int32
    dma = pltpu.SemaphoreType.DMA
    flops = 2 * depth * (2 * q_rows * (span + cycle) + span * pool_rows)
    in_vmem = pl.BlockSpec(memory_space=pltpu.VMEM)
    in_hbm = pl.BlockSpec(memory_space=pltpu.HBM)
    table, weights, loss = pl.pallas_call(
        functools.partial(kernel, n_blk),
        out_shape=(
            pltpu.VMEM((span + cycle, depth), bf16),
            pltpu.VMEM((q_rows, span + cycle), bf16),
            pltpu.VMEM((1, q_rows), f32),
        ),
        in_specs=[in_hbm] * 7,
        out_specs=(in_vmem,) * 3,
        scratch_shapes=[
            pltpu.VMEM((q_rows, depth), bf16),
            pltpu.VMEM((p_dev, depth), bf16),
            pltpu.VMEM((pool_rows, depth), bf16),
            pltpu.VMEM((1, q_rows), i32),
            pltpu.VMEM((owners, slots), i32),
            pltpu.VMEM((hn, q_rows), i32),
            pltpu.VMEM((1, q_rows), i32),
            pltpu.VMEM((span, pool_rows), bf16),
            pltpu.VMEM((span, pool_rows), bf16),
            pltpu.VMEM((span, depth), bf16),
            pltpu.VMEM((n_blk * TILE_ROWS, depth * p_dev // TILE_ROWS), bf16),
            dma((7,)), dma((4,)), dma((4,)), dma((4, CHUNKS)), dma((4, CHUNKS)),
            dma((n_blk,)), dma((n_blk,)),
        ],
        compiler_params=pltpu.CompilerParams(
            collective_id=0, has_side_effects=True, vmem_limit_bytes=VMEM_LIMIT),
        cost_estimate=pl.CostEstimate(
            flops=flops, bytes_accessed=4 * q_rows * depth, transcendentals=q_rows * (span + cycle)),
    )(*(pltpu.with_memory_space_constraint(x, pltpu.HBM) for x in (
        queries, passages, pool, positive_ids.reshape(1, q_rows), request_lists.reshape(owners, slots),
        hard_refs.T, hard_count.reshape(1, q_rows))))
    grad, loss = pl.pallas_call(
        grad_kernel,
        out_shape=(pltpu.HBM((q_rows, depth), bf16), pltpu.HBM((1, q_rows), f32)),
        in_specs=[in_vmem] * 3,
        out_specs=(in_hbm,) * 2,
        scratch_shapes=[pltpu.VMEM((q_rows, depth), bf16), dma((GRAD_TILES + 1,))],
        compiler_params=pltpu.CompilerParams(vmem_limit_bytes=VMEM_LIMIT),
        cost_estimate=pl.CostEstimate(
            flops=2 * depth * q_rows * (span + cycle), bytes_accessed=2 * q_rows * depth, transcendentals=0),
    )(table, weights, loss)
    return grad, loss.reshape(q_rows)


def solution(mesh):
    rows = P(("blk", "grp"), None)
    return jax.shard_map(
        functools.partial(body, mesh.shape["blk"]),
        mesh=mesh,
        in_specs=(rows, rows, rows, P(("blk", "grp")), P(("blk", "grp"), None, None), rows, P(("blk", "grp"))),
        out_specs=(rows, P(("blk", "grp"))),
        check_vma=False,
    )
```

```python
import functools

import jax
import jax.numpy as jnp
from jax import lax
from jax.experimental import pallas as pl
from jax.experimental.pallas import tpu as pltpu
from jax.sharding import PartitionSpec as P

MESH = pl.DeviceIdType.MESH
VMEM_LIMIT = 32 * 2**20
TILE_ROWS = 16
CHUNKS = 4


def iota(shape, axis):
    return lax.broadcasted_iota(jnp.int32, shape, axis)


def dot_nt(a, b):
    return lax.dot_general(a, b, (((1,), (1,)), ((), ())), preferred_element_type=jnp.float32)


def dot_nn(a, b):
    return jnp.dot(a, b, preferred_element_type=jnp.float32)


def kernel(n_blk, queries, passages, pool, positive, lists, refs, count, table, weights, loss,
           q_v, pass_v, pool_v, pos_v, list_v, refs_v, count_v,
           hot_out, hot_in, picked, packed,
           load_sem, hot_send, hot_recv, row_send, row_recv, pass_send, pass_recv, go_sem):
    blk = lax.axis_index("blk")
    grp = lax.axis_index("grp")
    q_rows, depth = q_v.shape
    p_dev = pass_v.shape[0]
    pool_rows = pool_v.shape[0]
    owners, slots = list_v.shape
    span = owners * slots
    cycle = n_blk * p_dev
    folds = TILE_ROWS // p_dev
    fold_w = depth // folds
    width = depth // CHUNKS

    half, core = lax.div(grp, 2), lax.rem(grp, 2)
    near, far_odd, far_even = half * 2 + 1 - core, (1 - half) * 2 + 1, (1 - half) * 2
    peers = (far_odd, far_even, near)
    is_hub = grp == 0

    barrier = pltpu.get_barrier_semaphore()
    for peer in peers:
        @pl.when(peer != 0)
        def _():
            pl.semaphore_signal(barrier, inc=1, device_id={"grp": peer}, device_id_type=MESH)

    loads = [
        pltpu.make_async_copy(src, dst, load_sem.at[i])
        for i, (src, dst) in enumerate((
            (lists, list_v), (passages, pass_v), (pool, pool_v), (refs, refs_v),
            (count, count_v), (positive, pos_v), (queries, q_v)))
    ]
    for load in loads:
        load.start()

    loads[0].wait()
    eye = iota((slots, slots), 0) == iota((slots, slots), 1)
    pool_iota = iota((slots, pool_rows), 1).astype(jnp.float32)
    wanted = list_v[...].astype(jnp.float32)
    for o in range(owners):
        column = jnp.sum(jnp.where(eye, wanted[o:o + 1, :], 0.0), axis=1, keepdims=True)
        hot_out[o * slots:(o + 1) * slots, :] = (pool_iota == column).astype(jnp.float32).astype(jnp.bfloat16)

    def slot_rows(owner):
        return pl.ds(pl.multiple_of(owner * slots, slots), slots)

    def hot_copy(source, target, peer):
        return pltpu.make_async_remote_copy(
            src_ref=hot_out.at[slot_rows(target)], dst_ref=hot_in.at[slot_rows(source)],
            send_sem=hot_send.at[target], recv_sem=hot_recv.at[source],
            device_id={"grp": peer}, device_id_type=MESH)

    def row_copy(source, target, c, peer):
        return pltpu.make_async_remote_copy(
            src_ref=picked.at[c, slot_rows(target)], dst_ref=table.at[c, slot_rows(source)],
            send_sem=row_send.at[target, c], recv_sem=row_recv.at[source, c],
            device_id={"grp": peer}, device_id_type=MESH)

    def pass_copy(step):
        return pltpu.make_async_remote_copy(
            src_ref=packed.at[own_slot], dst_ref=packed.at[own_slot],
            send_sem=pass_send.at[step], recv_sem=pass_recv.at[step],
            device_id={"blk": lax.rem(blk + step, n_blk)}, device_id_type=MESH)

    @pl.when(jnp.logical_not(is_hub))
    def _():
        pl.semaphore_wait(barrier, owners - 1)
        for peer in peers:
            hot_copy(grp, peer, peer).start()

    @pl.when(is_hub)
    def _():
        for peer in peers:
            hot_copy(peer, grp, peer).wait_recv()
        for peer in peers:
            hot_copy(grp, peer, peer).start()

        def greet(step, carry):
            pl.semaphore_signal(
                barrier, inc=1, device_id={"blk": lax.rem(blk + step, n_blk)}, device_id_type=MESH)
            return carry

        lax.fori_loop(1, n_blk, greet, 0)

    hot_in[slot_rows(grp), :] = hot_out[slot_rows(grp), :]

    def send_rows(c, first, last):
        rows = dot_nn(hot_in[first * slots:last * slots, :], pool_v[:, c * width:(c + 1) * width])
        picked[c, first * slots:last * slots, :] = rows.astype(jnp.bfloat16)
        for peer in reversed(range(first, last)):
            @pl.when(grp != peer)
            def _():
                row_copy(grp, peer, c, peer).start()

    def hot_arrived(peer):
        @pl.when(jnp.logical_and(jnp.logical_not(is_hub), grp != peer))
        def _():
            hot_copy(peer, grp, peer).wait_recv()

    loads[2].wait()
    for peer in range(1, owners):
        hot_arrived(peer)
    send_rows(0, 1, owners)
    send_rows(1, 1, owners)
    hot_arrived(0)
    for c in range(CHUNKS):
        send_rows(c, 0, 1)
        if c + 2 < CHUNKS:
            send_rows(c + 2, 1, owners)

    loads[1].wait()
    own = pass_v[...].astype(jnp.float32)
    fold_iota = iota((TILE_ROWS, fold_w), 0)
    folded = jnp.zeros((TILE_ROWS, fold_w), jnp.float32)
    for c in range(folds):
        for j in range(p_dev):
            folded = jnp.where(fold_iota == c * p_dev + j, own[j:j + 1, c * fold_w:(c + 1) * fold_w], folded)
    own_slot = pl.ds(pl.multiple_of(blk * TILE_ROWS, TILE_ROWS), TILE_ROWS)
    packed[own_slot, :] = folded.astype(jnp.bfloat16)

    @pl.when(is_hub)
    def _():
        pl.semaphore_wait(barrier, n_blk - 1)
        for peer in peers:
            pl.semaphore_signal(go_sem, inc=1, device_id={"grp": peer}, device_id_type=MESH)

    @pl.when(jnp.logical_not(is_hub))
    def _():
        pl.semaphore_wait(go_sem, 1)

    def send_pass(step, carry):
        pass_copy(step).start()
        return carry

    lax.fori_loop(1, n_blk, send_pass, 0)

    table[:, slot_rows(grp), :] = picked[:, slot_rows(grp), :]

    for load in loads[3:]:
        load.wait()
    hn = refs_v.shape[0]
    refs_t = jnp.where(iota((hn, q_rows), 0) < count_v[...], refs_v[...], -1)
    row_iota = iota((span, q_rows), 0)
    present = jnp.zeros((span, q_rows), jnp.float32)
    for i in range(hn):
        present = present + (row_iota == refs_t[i:i + 1, :]).astype(jnp.float32)

    def hard_part(c):
        cols = slice(c * width, (c + 1) * width)
        for peer in peers:
            row_copy(peer, grp, c, peer).wait_recv()
        return dot_nt(table[c, 0:span, :], q_v[:, cols])

    hard_logits = hard_part(0)
    for c in range(1, CHUNKS - 1):
        hard_logits = hard_logits + hard_part(c)

    def recv_pass(step, carry):
        pass_copy(step).wait()
        return carry

    lax.fori_loop(1, n_blk, recv_pass, 0)
    group_rows = folds * TILE_ROWS
    out_row, in_row = iota((group_rows, group_rows), 0), iota((group_rows, group_rows), 1)
    k = lax.rem(out_row, TILE_ROWS)
    source = lax.div(k, p_dev) * TILE_ROWS + lax.div(out_row, TILE_ROWS) * p_dev + lax.rem(k, p_dev)
    unfold = (source == in_row).astype(jnp.float32).astype(jnp.bfloat16)

    def unfold_group(i, carry):
        block = packed[pl.ds(pl.multiple_of(i * group_rows, group_rows), group_rows), :]
        rows = dot_nn(unfold, block).astype(jnp.bfloat16)
        place = pl.ds(pl.multiple_of(span + i * TILE_ROWS, TILE_ROWS), TILE_ROWS)
        for c in range(folds):
            at, within = divmod(c * fold_w, width)
            table[at, place, within:within + fold_w] = rows[c * TILE_ROWS:(c + 1) * TILE_ROWS, :]
        return carry

    lax.fori_loop(0, n_blk // folds, unfold_group, 0)
    cycle_logits = jnp.zeros((cycle, q_rows), jnp.float32)
    for c in range(CHUNKS):
        cols = slice(c * width, (c + 1) * width)
        cycle_logits = cycle_logits + dot_nt(table[c, span:span + cycle, :], q_v[:, cols])
    cycle_peak = jnp.max(cycle_logits, axis=0, keepdims=True)
    onehot = (iota((cycle, q_rows), 0) == pos_v[...]).astype(jnp.float32)
    chosen = jnp.sum(cycle_logits * onehot, axis=0, keepdims=True)

    hard_logits = hard_logits + hard_part(CHUNKS - 1)

    used = present > 0
    masked = jnp.where(used, hard_logits, -jnp.inf)
    peak = jnp.maximum(cycle_peak, jnp.max(masked, axis=0, keepdims=True))
    cycle_exp = jnp.exp(cycle_logits - peak)
    hard_exp = present * jnp.exp(jnp.where(used, hard_logits - peak, 0.0))
    denominator = jnp.sum(cycle_exp, axis=0, keepdims=True) + jnp.sum(hard_exp, axis=0, keepdims=True)
    loss[...] = jnp.log(denominator) + peak - chosen
    scale = 1.0 / denominator
    weights[:, 0:span] = (hard_exp * scale).T.astype(jnp.bfloat16)
    weights[:, span:span + cycle] = (cycle_exp * scale - onehot).T.astype(jnp.bfloat16)

    for peer in peers:
        hot_copy(grp, peer, peer).wait_send()
        for c in range(CHUNKS):
            row_copy(grp, peer, c, peer).wait_send()


def grad_kernel(table, weights, loss, grad, loss_out, grad_v, sems):
    tiles, _, width = table.shape
    copies = [pltpu.make_async_copy(loss, loss_out, sems.at[tiles])]
    copies[0].start()
    for c in range(tiles):
        cols = slice(c * width, (c + 1) * width)
        grad_v[:, cols] = dot_nn(weights[...], table[c]).astype(jnp.bfloat16)
        here = pl.ds(c * width, width)
        copies.append(pltpu.make_async_copy(grad_v.at[:, here], grad.at[:, here], sems.at[c]))
        copies[-1].start()
    for copy in copies:
        copy.wait()


def body(n_blk, queries, passages, pool, positive_ids, request_lists, hard_refs, hard_count):
    q_rows, depth = queries.shape
    p_dev = passages.shape[0]
    pool_rows = pool.shape[0]
    _, owners, slots = request_lists.shape
    hn = hard_refs.shape[1]
    span, cycle = owners * slots, n_blk * p_dev
    width = depth // CHUNKS
    bf16, f32, i32 = jnp.bfloat16, jnp.float32, jnp.int32
    dma = pltpu.SemaphoreType.DMA
    flops = 2 * depth * (2 * q_rows * (span + cycle) + span * pool_rows)
    in_vmem = pl.BlockSpec(memory_space=pltpu.VMEM)
    in_hbm = pl.BlockSpec(memory_space=pltpu.HBM)
    table, weights, loss = pl.pallas_call(
        functools.partial(kernel, n_blk),
        out_shape=(
            pltpu.VMEM((CHUNKS, span + cycle, width), bf16),
            pltpu.VMEM((q_rows, span + cycle), bf16),
            pltpu.VMEM((1, q_rows), f32),
        ),
        in_specs=[in_hbm] * 7,
        out_specs=(in_vmem,) * 3,
        scratch_shapes=[
            pltpu.VMEM((q_rows, depth), bf16),
            pltpu.VMEM((p_dev, depth), bf16),
            pltpu.VMEM((pool_rows, depth), bf16),
            pltpu.VMEM((1, q_rows), i32),
            pltpu.VMEM((owners, slots), i32),
            pltpu.VMEM((hn, q_rows), i32),
            pltpu.VMEM((1, q_rows), i32),
            pltpu.VMEM((span, pool_rows), bf16),
            pltpu.VMEM((span, pool_rows), bf16),
            pltpu.VMEM((CHUNKS, span, width), bf16),
            pltpu.VMEM((n_blk * TILE_ROWS, depth * p_dev // TILE_ROWS), bf16),
            dma((7,)), dma((owners,)), dma((owners,)), dma((owners, CHUNKS)), dma((owners, CHUNKS)),
            dma((n_blk,)), dma((n_blk,)), pltpu.SemaphoreType.REGULAR,
        ],
        compiler_params=pltpu.CompilerParams(
            collective_id=0, has_side_effects=True, vmem_limit_bytes=VMEM_LIMIT),
        cost_estimate=pl.CostEstimate(
            flops=flops, bytes_accessed=4 * q_rows * depth, transcendentals=q_rows * (span + cycle)),
    )(*(pltpu.with_memory_space_constraint(x, pltpu.HBM) for x in (
        queries, passages, pool, positive_ids.reshape(1, q_rows), request_lists.reshape(owners, slots),
        hard_refs.T, hard_count.reshape(1, q_rows))))
    grad, loss = pl.pallas_call(
        grad_kernel,
        out_shape=(pltpu.HBM((q_rows, depth), bf16), pltpu.HBM((1, q_rows), f32)),
        in_specs=[in_vmem] * 3,
        out_specs=(in_hbm,) * 2,
        scratch_shapes=[pltpu.VMEM((q_rows, depth), bf16), dma((CHUNKS + 1,))],
        compiler_params=pltpu.CompilerParams(vmem_limit_bytes=VMEM_LIMIT),
        cost_estimate=pl.CostEstimate(
            flops=2 * depth * q_rows * (span + cycle), bytes_accessed=2 * q_rows * depth, transcendentals=0),
    )(table, weights, loss)
    return grad, loss.reshape(q_rows)


def solution(mesh):
    rows = P(("blk", "grp"), None)
    return jax.shard_map(
        functools.partial(body, mesh.shape["blk"]),
        mesh=mesh,
        in_specs=(rows, rows, rows, P(("blk", "grp")), P(("blk", "grp"), None, None), rows, P(("blk", "grp"))),
        out_specs=(rows, P(("blk", "grp"))),
        check_vma=False,
    )
```

```python
import functools

import jax
import jax.numpy as jnp
from jax import lax
from jax.experimental import pallas as pl
from jax.experimental.pallas import tpu as pltpu
from jax.sharding import PartitionSpec as P

MESH = pl.DeviceIdType.MESH
VMEM_LIMIT = 32 * 2**20
TILE_ROWS = 16
CHUNKS = 4


def iota(shape, axis):
    return lax.broadcasted_iota(jnp.int32, shape, axis)


def dot_nt(a, b):
    return lax.dot_general(a, b, (((1,), (1,)), ((), ())), preferred_element_type=jnp.float32)


def dot_nn(a, b):
    return jnp.dot(a, b, preferred_element_type=jnp.float32)


def kernel(n_blk, queries, passages, pool, positive, lists, refs, count, table, weights, loss,
           q_v, pass_v, pool_v, pos_v, list_v, refs_v, count_v,
           hot_out, hot_in, picked, packed,
           load_sem, hot_send, hot_recv, row_send, row_recv, pass_send, pass_recv, go_sem):
    blk = lax.axis_index("blk")
    grp = lax.axis_index("grp")
    q_rows, depth = q_v.shape
    p_dev = pass_v.shape[0]
    pool_rows = pool_v.shape[0]
    owners, slots = list_v.shape
    span = owners * slots
    cycle = n_blk * p_dev
    folds = TILE_ROWS // p_dev
    fold_w = depth // folds
    width = depth // CHUNKS

    half, core = lax.div(grp, 2), lax.rem(grp, 2)
    near, far_odd, far_even = half * 2 + 1 - core, (1 - half) * 2 + 1, (1 - half) * 2
    peers = (far_odd, far_even, near)
    is_hub = grp == 0

    barrier = pltpu.get_barrier_semaphore()
    for peer in peers:
        @pl.when(peer != 0)
        def _():
            pl.semaphore_signal(barrier, inc=1, device_id={"grp": peer}, device_id_type=MESH)

    loads = [
        pltpu.make_async_copy(src, dst, load_sem.at[i])
        for i, (src, dst) in enumerate((
            (lists, list_v), (passages, pass_v), (pool, pool_v), (refs, refs_v),
            (count, count_v), (positive, pos_v), (queries, q_v)))
    ]
    for load in loads:
        load.start()

    loads[0].wait()
    eye = iota((slots, slots), 0) == iota((slots, slots), 1)
    pool_iota = iota((slots, pool_rows), 1).astype(jnp.float32)
    wanted = list_v[...].astype(jnp.float32)
    for o in range(owners):
        column = jnp.sum(jnp.where(eye, wanted[o:o + 1, :], 0.0), axis=1, keepdims=True)
        hot_out[o * slots:(o + 1) * slots, :] = (pool_iota == column).astype(jnp.float32).astype(jnp.bfloat16)

    def slot_rows(owner):
        return pl.ds(pl.multiple_of(owner * slots, slots), slots)

    def hot_copy(source, target, peer):
        return pltpu.make_async_remote_copy(
            src_ref=hot_out.at[slot_rows(target)], dst_ref=hot_in.at[slot_rows(source)],
            send_sem=hot_send.at[target], recv_sem=hot_recv.at[source],
            device_id={"grp": peer}, device_id_type=MESH)

    def row_copy(source, target, c, peer):
        return pltpu.make_async_remote_copy(
            src_ref=picked.at[c, slot_rows(target)], dst_ref=table.at[c, slot_rows(source)],
            send_sem=row_send.at[target, c], recv_sem=row_recv.at[source, c],
            device_id={"grp": peer}, device_id_type=MESH)

    def pass_copy(step):
        return pltpu.make_async_remote_copy(
            src_ref=packed.at[own_slot], dst_ref=packed.at[own_slot],
            send_sem=pass_send.at[step], recv_sem=pass_recv.at[step],
            device_id={"blk": lax.rem(blk + step, n_blk)}, device_id_type=MESH)

    @pl.when(jnp.logical_not(is_hub))
    def _():
        pl.semaphore_wait(barrier, owners - 1)
        for peer in peers:
            hot_copy(grp, peer, peer).start()

    @pl.when(is_hub)
    def _():
        for peer in peers:
            hot_copy(peer, grp, peer).wait_recv()
        for peer in peers:
            hot_copy(grp, peer, peer).start()

        def greet(step, carry):
            pl.semaphore_signal(
                barrier, inc=1, device_id={"blk": lax.rem(blk + step, n_blk)}, device_id_type=MESH)
            return carry

        lax.fori_loop(1, n_blk, greet, 0)

    loads[1].wait()
    own = pass_v[...].astype(jnp.float32)
    fold_iota = iota((TILE_ROWS, fold_w), 0)
    folded = jnp.zeros((TILE_ROWS, fold_w), jnp.float32)
    for c in range(folds):
        for j in range(p_dev):
            folded = jnp.where(fold_iota == c * p_dev + j, own[j:j + 1, c * fold_w:(c + 1) * fold_w], folded)
    own_slot = pl.ds(pl.multiple_of(blk * TILE_ROWS, TILE_ROWS), TILE_ROWS)
    packed[own_slot, :] = folded.astype(jnp.bfloat16)

    hot_in[slot_rows(grp), :] = hot_out[slot_rows(grp), :]

    def pick_rows(c, first, last):
        rows = dot_nn(hot_in[first * slots:last * slots, :], pool_v[:, c * width:(c + 1) * width])
        picked[c, first * slots:last * slots, :] = rows.astype(jnp.bfloat16)
        for peer in range(first, last):
            @pl.when(half != peer // 2)
            def _():
                row_copy(grp, peer, c, peer).start()

    def hot_arrived(peer):
        @pl.when(jnp.logical_and(jnp.logical_not(is_hub), grp != peer))
        def _():
            hot_copy(peer, grp, peer).wait_recv()

    loads[2].wait()
    for peer in range(1, owners):
        hot_arrived(peer)
    pick_rows(0, 1, owners)
    hot_arrived(0)
    pick_rows(0, 0, 1)
    ahead = CHUNKS // 2
    for c in range(1, CHUNKS):
        if c < ahead:
            pick_rows(c, 1, owners)
            pick_rows(c, 0, 1)
        else:
            pick_rows(c, 0, 1)
            pick_rows(c, 1, owners)
    for c in range(CHUNKS):
        row_copy(grp, near, c, near).start()

    @pl.when(is_hub)
    def _():
        pl.semaphore_wait(barrier, n_blk - 1)
        for peer in peers:
            pl.semaphore_signal(go_sem, inc=1, device_id={"grp": peer}, device_id_type=MESH)

    @pl.when(jnp.logical_not(is_hub))
    def _():
        pl.semaphore_wait(go_sem, 1)

    def send_pass(step, carry):
        pass_copy(step).start()
        return carry

    lax.fori_loop(1, n_blk, send_pass, 0)

    table[:, slot_rows(grp), :] = picked[:, slot_rows(grp), :]

    for load in loads[3:]:
        load.wait()
    hn = refs_v.shape[0]
    refs_t = jnp.where(iota((hn, q_rows), 0) < count_v[...], refs_v[...], -1)
    row_iota = iota((span, q_rows), 0)
    present = jnp.zeros((span, q_rows), jnp.float32)
    for i in range(hn):
        present = present + (row_iota == refs_t[i:i + 1, :]).astype(jnp.float32)

    def hard_part(c):
        cols = slice(c * width, (c + 1) * width)
        for peer in peers:
            row_copy(peer, grp, c, peer).wait_recv()
        return dot_nt(table[c, 0:span, :], q_v[:, cols])

    hard_logits = hard_part(0)
    for c in range(1, CHUNKS - 1):
        hard_logits = hard_logits + hard_part(c)

    def recv_pass(step, carry):
        pass_copy(step).wait()
        return carry

    lax.fori_loop(1, n_blk, recv_pass, 0)
    group_rows = folds * TILE_ROWS
    out_row, in_row = iota((group_rows, group_rows), 0), iota((group_rows, group_rows), 1)
    k = lax.rem(out_row, TILE_ROWS)
    source = lax.div(k, p_dev) * TILE_ROWS + lax.div(out_row, TILE_ROWS) * p_dev + lax.rem(k, p_dev)
    unfold = (source == in_row).astype(jnp.float32).astype(jnp.bfloat16)

    def unfold_group(i, carry):
        block = packed[pl.ds(pl.multiple_of(i * group_rows, group_rows), group_rows), :]
        rows = dot_nn(unfold, block).astype(jnp.bfloat16)
        place = pl.ds(pl.multiple_of(span + i * TILE_ROWS, TILE_ROWS), TILE_ROWS)
        for c in range(folds):
            at, within = divmod(c * fold_w, width)
            table[at, place, within:within + fold_w] = rows[c * TILE_ROWS:(c + 1) * TILE_ROWS, :]
        return carry

    lax.fori_loop(0, n_blk // folds, unfold_group, 0)
    cycle_logits = jnp.zeros((cycle, q_rows), jnp.float32)
    for c in range(CHUNKS):
        cols = slice(c * width, (c + 1) * width)
        cycle_logits = cycle_logits + dot_nt(table[c, span:span + cycle, :], q_v[:, cols])
    cycle_peak = jnp.max(cycle_logits, axis=0, keepdims=True)
    onehot = (iota((cycle, q_rows), 0) == pos_v[...]).astype(jnp.float32)
    chosen = jnp.sum(cycle_logits * onehot, axis=0, keepdims=True)

    hard_logits = hard_logits + hard_part(CHUNKS - 1)

    used = present > 0
    masked = jnp.where(used, hard_logits, -jnp.inf)
    peak = jnp.maximum(cycle_peak, jnp.max(masked, axis=0, keepdims=True))
    cycle_exp = jnp.exp(cycle_logits - peak)
    hard_exp = present * jnp.exp(jnp.where(used, hard_logits - peak, 0.0))
    denominator = jnp.sum(cycle_exp, axis=0, keepdims=True) + jnp.sum(hard_exp, axis=0, keepdims=True)
    loss[...] = jnp.log(denominator) + peak - chosen
    scale = 1.0 / denominator
    weights[:, 0:span] = (hard_exp * scale).T.astype(jnp.bfloat16)
    weights[:, span:span + cycle] = (cycle_exp * scale - onehot).T.astype(jnp.bfloat16)

    for peer in peers:
        hot_copy(grp, peer, peer).wait_send()
        for c in range(CHUNKS):
            row_copy(grp, peer, c, peer).wait_send()


def grad_kernel(table, weights, loss, grad, loss_out, grad_v, sems):
    tiles, _, width = table.shape
    copies = [pltpu.make_async_copy(loss, loss_out, sems.at[tiles])]
    copies[0].start()
    for c in range(tiles):
        cols = slice(c * width, (c + 1) * width)
        grad_v[:, cols] = dot_nn(weights[...], table[c]).astype(jnp.bfloat16)
        here = pl.ds(c * width, width)
        copies.append(pltpu.make_async_copy(grad_v.at[:, here], grad.at[:, here], sems.at[c]))
        copies[-1].start()
    for copy in copies:
        copy.wait()


def body(n_blk, queries, passages, pool, positive_ids, request_lists, hard_refs, hard_count):
    q_rows, depth = queries.shape
    p_dev = passages.shape[0]
    pool_rows = pool.shape[0]
    _, owners, slots = request_lists.shape
    hn = hard_refs.shape[1]
    span, cycle = owners * slots, n_blk * p_dev
    width = depth // CHUNKS
    bf16, f32, i32 = jnp.bfloat16, jnp.float32, jnp.int32
    dma = pltpu.SemaphoreType.DMA
    flops = 2 * depth * (2 * q_rows * (span + cycle) + span * pool_rows)
    in_vmem = pl.BlockSpec(memory_space=pltpu.VMEM)
    in_hbm = pl.BlockSpec(memory_space=pltpu.HBM)
    table, weights, loss = pl.pallas_call(
        functools.partial(kernel, n_blk),
        out_shape=(
            pltpu.VMEM((CHUNKS, span + cycle, width), bf16),
            pltpu.VMEM((q_rows, span + cycle), bf16),
            pltpu.VMEM((1, q_rows), f32),
        ),
        in_specs=[in_hbm] * 7,
        out_specs=(in_vmem,) * 3,
        scratch_shapes=[
            pltpu.VMEM((q_rows, depth), bf16),
            pltpu.VMEM((p_dev, depth), bf16),
            pltpu.VMEM((pool_rows, depth), bf16),
            pltpu.VMEM((1, q_rows), i32),
            pltpu.VMEM((owners, slots), i32),
            pltpu.VMEM((hn, q_rows), i32),
            pltpu.VMEM((1, q_rows), i32),
            pltpu.VMEM((span, pool_rows), bf16),
            pltpu.VMEM((span, pool_rows), bf16),
            pltpu.VMEM((CHUNKS, span, width), bf16),
            pltpu.VMEM((n_blk * TILE_ROWS, depth * p_dev // TILE_ROWS), bf16),
            dma((7,)), dma((owners,)), dma((owners,)), dma((owners, CHUNKS)), dma((owners, CHUNKS)),
            dma((n_blk,)), dma((n_blk,)), pltpu.SemaphoreType.REGULAR,
        ],
        compiler_params=pltpu.CompilerParams(
            collective_id=0, has_side_effects=True, vmem_limit_bytes=VMEM_LIMIT),
        cost_estimate=pl.CostEstimate(
            flops=flops, bytes_accessed=4 * q_rows * depth, transcendentals=q_rows * (span + cycle)),
    )(*(pltpu.with_memory_space_constraint(x, pltpu.HBM) for x in (
        queries, passages, pool, positive_ids.reshape(1, q_rows), request_lists.reshape(owners, slots),
        hard_refs.T, hard_count.reshape(1, q_rows))))
    grad, loss = pl.pallas_call(
        grad_kernel,
        out_shape=(pltpu.HBM((q_rows, depth), bf16), pltpu.HBM((1, q_rows), f32)),
        in_specs=[in_vmem] * 3,
        out_specs=(in_hbm,) * 2,
        scratch_shapes=[pltpu.VMEM((q_rows, depth), bf16), dma((CHUNKS + 1,))],
        compiler_params=pltpu.CompilerParams(vmem_limit_bytes=VMEM_LIMIT),
        cost_estimate=pl.CostEstimate(
            flops=2 * depth * q_rows * (span + cycle), bytes_accessed=2 * q_rows * depth, transcendentals=0),
    )(table, weights, loss)
    return grad, loss.reshape(q_rows)


def solution(mesh):
    rows = P(("blk", "grp"), None)
    return jax.shard_map(
        functools.partial(body, mesh.shape["blk"]),
        mesh=mesh,
        in_specs=(rows, rows, rows, P(("blk", "grp")), P(("blk", "grp"), None, None), rows, P(("blk", "grp"))),
        out_specs=(rows, P(("blk", "grp"))),
        check_vma=False,
    )
```

```python
import functools

import jax
import jax.numpy as jnp
from jax import lax
from jax.experimental import pallas as pl
from jax.experimental.pallas import tpu as pltpu
from jax.sharding import PartitionSpec as P

MESH = pl.DeviceIdType.MESH
VMEM_LIMIT = 32 * 2**20
TILE_ROWS = 16
CHUNKS = 4


def iota(shape, axis):
    return lax.broadcasted_iota(jnp.int32, shape, axis)


def dot_nt(a, b):
    return lax.dot_general(a, b, (((1,), (1,)), ((), ())), preferred_element_type=jnp.float32)


def dot_nn(a, b):
    return jnp.dot(a, b, preferred_element_type=jnp.float32)


def kernel(n_blk, queries, passages, pool, positive, lists, refs, count, table, weights, loss,
           q_v, pass_v, pool_v, pos_v, list_v, refs_v, count_v,
           hot_out, hot_in, picked, packed,
           load_sem, hot_send, hot_recv, row_send, row_recv, pass_send, pass_recv, go_sem):
    blk = lax.axis_index("blk")
    grp = lax.axis_index("grp")
    q_rows, depth = q_v.shape
    p_dev = pass_v.shape[0]
    pool_rows = pool_v.shape[0]
    owners, slots = list_v.shape
    span = owners * slots
    cycle = n_blk * p_dev
    folds = TILE_ROWS // p_dev
    fold_w = depth // folds
    width = depth // CHUNKS

    half, core = lax.div(grp, 2), lax.rem(grp, 2)
    near, far_odd, far_even = half * 2 + 1 - core, (1 - half) * 2 + 1, (1 - half) * 2
    peers = (far_odd, far_even, near)
    is_hub = grp == 0

    barrier = pltpu.get_barrier_semaphore()
    for peer in peers:
        @pl.when(peer != 0)
        def _():
            pl.semaphore_signal(barrier, inc=1, device_id={"grp": peer}, device_id_type=MESH)

    loads = [
        pltpu.make_async_copy(src, dst, load_sem.at[i])
        for i, (src, dst) in enumerate((
            (lists, list_v), (passages, pass_v), (pool, pool_v), (refs, refs_v),
            (count, count_v), (positive, pos_v), (queries, q_v)))
    ]
    for load in loads:
        load.start()

    loads[0].wait()
    eye = iota((slots, slots), 0) == iota((slots, slots), 1)
    pool_iota = iota((slots, pool_rows), 1).astype(jnp.float32)
    wanted = list_v[...].astype(jnp.float32)
    for o in range(owners):
        column = jnp.sum(jnp.where(eye, wanted[o:o + 1, :], 0.0), axis=1, keepdims=True)
        hot_out[o * slots:(o + 1) * slots, :] = (pool_iota == column).astype(jnp.float32).astype(jnp.bfloat16)

    def slot_rows(owner):
        return pl.ds(pl.multiple_of(owner * slots, slots), slots)

    def hot_copy(source, target, peer):
        return pltpu.make_async_remote_copy(
            src_ref=hot_out.at[slot_rows(target)], dst_ref=hot_in.at[slot_rows(source)],
            send_sem=hot_send.at[target], recv_sem=hot_recv.at[source],
            device_id={"grp": peer}, device_id_type=MESH)

    def row_copy(source, target, c, peer):
        return pltpu.make_async_remote_copy(
            src_ref=picked.at[c, slot_rows(target)], dst_ref=table.at[c, slot_rows(source)],
            send_sem=row_send.at[target, c], recv_sem=row_recv.at[source, c],
            device_id={"grp": peer}, device_id_type=MESH)

    def pass_copy(step):
        return pltpu.make_async_remote_copy(
            src_ref=packed.at[own_slot], dst_ref=packed.at[own_slot],
            send_sem=pass_send.at[step], recv_sem=pass_recv.at[step],
            device_id={"blk": lax.rem(blk + step, n_blk)}, device_id_type=MESH)

    @pl.when(jnp.logical_not(is_hub))
    def _():
        pl.semaphore_wait(barrier, owners - 1)
        for peer in peers:
            hot_copy(grp, peer, peer).start()

    @pl.when(is_hub)
    def _():
        for peer in peers:
            hot_copy(peer, grp, peer).wait_recv()
        for peer in peers:
            hot_copy(grp, peer, peer).start()

        def greet(step, carry):
            pl.semaphore_signal(
                barrier, inc=1, device_id={"blk": lax.rem(blk + step, n_blk)}, device_id_type=MESH)
            return carry

        lax.fori_loop(1, n_blk, greet, 0)

    loads[1].wait()
    own = pass_v[...].astype(jnp.float32)
    fold_iota = iota((TILE_ROWS, fold_w), 0)
    folded = jnp.zeros((TILE_ROWS, fold_w), jnp.float32)
    for c in range(folds):
        for j in range(p_dev):
            folded = jnp.where(fold_iota == c * p_dev + j, own[j:j + 1, c * fold_w:(c + 1) * fold_w], folded)
    own_slot = pl.ds(pl.multiple_of(blk * TILE_ROWS, TILE_ROWS), TILE_ROWS)
    packed[own_slot, :] = folded.astype(jnp.bfloat16)

    hot_in[slot_rows(grp), :] = hot_out[slot_rows(grp), :]

    def pick_rows(c, first, last):
        rows = dot_nn(hot_in[first * slots:last * slots, :], pool_v[:, c * width:(c + 1) * width])
        picked[c, first * slots:last * slots, :] = rows.astype(jnp.bfloat16)
        for peer in range(first, last):
            @pl.when(half != peer // 2)
            def _():
                row_copy(grp, peer, c, peer).start()

    def hot_arrived(peer):
        @pl.when(jnp.logical_and(jnp.logical_not(is_hub), grp != peer))
        def _():
            hot_copy(peer, grp, peer).wait_recv()

    loads[2].wait()
    for peer in range(1, owners):
        hot_arrived(peer)
    for c in range(CHUNKS):
        pick_rows(c, 1, owners)
    hot_arrived(0)
    for c in range(CHUNKS):
        pick_rows(c, 0, 1)
    for c in range(CHUNKS):
        row_copy(grp, near, c, near).start()

    @pl.when(is_hub)
    def _():
        pl.semaphore_wait(barrier, n_blk - 1)
        for peer in peers:
            pl.semaphore_signal(go_sem, inc=1, device_id={"grp": peer}, device_id_type=MESH)

    @pl.when(jnp.logical_not(is_hub))
    def _():
        pl.semaphore_wait(go_sem, 1)

    def send_pass(step, carry):
        pass_copy(step).start()
        return carry

    lax.fori_loop(1, n_blk, send_pass, 0)

    table[:, slot_rows(grp), :] = picked[:, slot_rows(grp), :]

    for load in loads[3:]:
        load.wait()
    hn = refs_v.shape[0]
    refs_t = jnp.where(iota((hn, q_rows), 0) < count_v[...], refs_v[...], -1)
    row_iota = iota((span, q_rows), 0)
    present = jnp.zeros((span, q_rows), jnp.float32)
    for i in range(hn):
        present = present + (row_iota == refs_t[i:i + 1, :]).astype(jnp.float32)

    def hard_part(c):
        cols = slice(c * width, (c + 1) * width)
        for peer in peers:
            row_copy(peer, grp, c, peer).wait_recv()
        return dot_nt(table[c, 0:span, :], q_v[:, cols])

    hard_logits = hard_part(0)
    for c in range(1, CHUNKS - 1):
        hard_logits = hard_logits + hard_part(c)

    def recv_pass(step, carry):
        pass_copy(step).wait()
        return carry

    lax.fori_loop(1, n_blk, recv_pass, 0)
    group_rows = folds * TILE_ROWS
    out_row, in_row = iota((group_rows, group_rows), 0), iota((group_rows, group_rows), 1)
    k = lax.rem(out_row, TILE_ROWS)
    source = lax.div(k, p_dev) * TILE_ROWS + lax.div(out_row, TILE_ROWS) * p_dev + lax.rem(k, p_dev)
    unfold = (source == in_row).astype(jnp.float32).astype(jnp.bfloat16)

    def unfold_group(i, carry):
        block = packed[pl.ds(pl.multiple_of(i * group_rows, group_rows), group_rows), :]
        rows = dot_nn(unfold, block).astype(jnp.bfloat16)
        place = pl.ds(pl.multiple_of(span + i * TILE_ROWS, TILE_ROWS), TILE_ROWS)
        for c in range(folds):
            at, within = divmod(c * fold_w, width)
            table[at, place, within:within + fold_w] = rows[c * TILE_ROWS:(c + 1) * TILE_ROWS, :]
        return carry

    lax.fori_loop(0, n_blk // folds, unfold_group, 0)
    cycle_logits = jnp.zeros((cycle, q_rows), jnp.float32)
    for c in range(CHUNKS):
        cols = slice(c * width, (c + 1) * width)
        cycle_logits = cycle_logits + dot_nt(table[c, span:span + cycle, :], q_v[:, cols])
    cycle_peak = jnp.max(cycle_logits, axis=0, keepdims=True)
    onehot = (iota((cycle, q_rows), 0) == pos_v[...]).astype(jnp.float32)
    chosen = jnp.sum(cycle_logits * onehot, axis=0, keepdims=True)

    hard_logits = hard_logits + hard_part(CHUNKS - 1)

    used = present > 0
    masked = jnp.where(used, hard_logits, -jnp.inf)
    peak = jnp.maximum(cycle_peak, jnp.max(masked, axis=0, keepdims=True))
    cycle_exp = jnp.exp(cycle_logits - peak)
    hard_exp = present * jnp.exp(jnp.where(used, hard_logits - peak, 0.0))
    denominator = jnp.sum(cycle_exp, axis=0, keepdims=True) + jnp.sum(hard_exp, axis=0, keepdims=True)
    loss[...] = jnp.log(denominator) + peak - chosen
    scale = 1.0 / denominator
    weights[:, 0:span] = (hard_exp * scale).T.astype(jnp.bfloat16)
    weights[:, span:span + cycle] = (cycle_exp * scale - onehot).T.astype(jnp.bfloat16)

    for peer in peers:
        hot_copy(grp, peer, peer).wait_send()
        for c in range(CHUNKS):
            row_copy(grp, peer, c, peer).wait_send()


def grad_kernel(table, weights, loss, grad, loss_out, grad_v, sems):
    tiles, _, width = table.shape
    copies = [pltpu.make_async_copy(loss, loss_out, sems.at[tiles])]
    copies[0].start()
    for c in range(tiles):
        cols = slice(c * width, (c + 1) * width)
        grad_v[:, cols] = dot_nn(weights[...], table[c]).astype(jnp.bfloat16)
        here = pl.ds(c * width, width)
        copies.append(pltpu.make_async_copy(grad_v.at[:, here], grad.at[:, here], sems.at[c]))
        copies[-1].start()
    for copy in copies:
        copy.wait()


def body(n_blk, queries, passages, pool, positive_ids, request_lists, hard_refs, hard_count):
    q_rows, depth = queries.shape
    p_dev = passages.shape[0]
    pool_rows = pool.shape[0]
    _, owners, slots = request_lists.shape
    hn = hard_refs.shape[1]
    span, cycle = owners * slots, n_blk * p_dev
    width = depth // CHUNKS
    bf16, f32, i32 = jnp.bfloat16, jnp.float32, jnp.int32
    dma = pltpu.SemaphoreType.DMA
    flops = 2 * depth * (2 * q_rows * (span + cycle) + span * pool_rows)
    in_vmem = pl.BlockSpec(memory_space=pltpu.VMEM)
    in_hbm = pl.BlockSpec(memory_space=pltpu.HBM)
    table, weights, loss = pl.pallas_call(
        functools.partial(kernel, n_blk),
        out_shape=(
            pltpu.VMEM((CHUNKS, span + cycle, width), bf16),
            pltpu.VMEM((q_rows, span + cycle), bf16),
            pltpu.VMEM((1, q_rows), f32),
        ),
        in_specs=[in_hbm] * 7,
        out_specs=(in_vmem,) * 3,
        scratch_shapes=[
            pltpu.VMEM((q_rows, depth), bf16),
            pltpu.VMEM((p_dev, depth), bf16),
            pltpu.VMEM((pool_rows, depth), bf16),
            pltpu.VMEM((1, q_rows), i32),
            pltpu.VMEM((owners, slots), i32),
            pltpu.VMEM((hn, q_rows), i32),
            pltpu.VMEM((1, q_rows), i32),
            pltpu.VMEM((span, pool_rows), bf16),
            pltpu.VMEM((span, pool_rows), bf16),
            pltpu.VMEM((CHUNKS, span, width), bf16),
            pltpu.VMEM((n_blk * TILE_ROWS, depth * p_dev // TILE_ROWS), bf16),
            dma((7,)), dma((owners,)), dma((owners,)), dma((owners, CHUNKS)), dma((owners, CHUNKS)),
            dma((n_blk,)), dma((n_blk,)), pltpu.SemaphoreType.REGULAR,
        ],
        compiler_params=pltpu.CompilerParams(
            collective_id=0, has_side_effects=True, vmem_limit_bytes=VMEM_LIMIT),
        cost_estimate=pl.CostEstimate(
            flops=flops, bytes_accessed=4 * q_rows * depth, transcendentals=q_rows * (span + cycle)),
    )(*(pltpu.with_memory_space_constraint(x, pltpu.HBM) for x in (
        queries, passages, pool, positive_ids.reshape(1, q_rows), request_lists.reshape(owners, slots),
        hard_refs.T, hard_count.reshape(1, q_rows))))
    grad, loss = pl.pallas_call(
        grad_kernel,
        out_shape=(pltpu.HBM((q_rows, depth), bf16), pltpu.HBM((1, q_rows), f32)),
        in_specs=[in_vmem] * 3,
        out_specs=(in_hbm,) * 2,
        scratch_shapes=[pltpu.VMEM((q_rows, depth), bf16), dma((CHUNKS + 1,))],
        compiler_params=pltpu.CompilerParams(vmem_limit_bytes=VMEM_LIMIT),
        cost_estimate=pl.CostEstimate(
            flops=2 * depth * q_rows * (span + cycle), bytes_accessed=2 * q_rows * depth, transcendentals=0),
    )(table, weights, loss)
    return grad, loss.reshape(q_rows)


def solution(mesh):
    rows = P(("blk", "grp"), None)
    return jax.shard_map(
        functools.partial(body, mesh.shape["blk"]),
        mesh=mesh,
        in_specs=(rows, rows, rows, P(("blk", "grp")), P(("blk", "grp"), None, None), rows, P(("blk", "grp"))),
        out_specs=(rows, P(("blk", "grp"))),
        check_vma=False,
    )
```

```python
import functools

import jax
import jax.numpy as jnp
from jax import lax
from jax.experimental import pallas as pl
from jax.experimental.pallas import tpu as pltpu
from jax.sharding import PartitionSpec as P

MESH = pl.DeviceIdType.MESH
VMEM_LIMIT = 32 * 2**20
TILE_ROWS = 16
CHUNKS = 4


def iota(shape, axis):
    return lax.broadcasted_iota(jnp.int32, shape, axis)


def dot_nt(a, b):
    return lax.dot_general(a, b, (((1,), (1,)), ((), ())), preferred_element_type=jnp.float32)


def dot_nn(a, b):
    return jnp.dot(a, b, preferred_element_type=jnp.float32)


def kernel(n_blk, queries, passages, pool, positive, lists, refs, count, table, weights, loss,
           q_v, pass_v, pool_v, pos_v, list_v, refs_v, count_v,
           hot_out, hot_in, picked, packed,
           load_sem, hot_send, hot_recv, row_send, row_recv, pass_send, pass_recv, go_sem):
    blk = lax.axis_index("blk")
    grp = lax.axis_index("grp")
    q_rows, depth = q_v.shape
    p_dev = pass_v.shape[0]
    pool_rows = pool_v.shape[0]
    owners, slots = list_v.shape
    span = owners * slots
    cycle = n_blk * p_dev
    folds = TILE_ROWS // p_dev
    fold_w = depth // folds
    width = depth // CHUNKS

    half, core = lax.div(grp, 2), lax.rem(grp, 2)
    near, far_odd, far_even = half * 2 + 1 - core, (1 - half) * 2 + 1, (1 - half) * 2
    peers = (far_odd, far_even, near)
    is_hub = grp == 0

    barrier = pltpu.get_barrier_semaphore()
    for peer in peers:
        @pl.when(peer != 0)
        def _():
            pl.semaphore_signal(barrier, inc=1, device_id={"grp": peer}, device_id_type=MESH)

    loads = [
        pltpu.make_async_copy(src, dst, load_sem.at[i])
        for i, (src, dst) in enumerate((
            (lists, list_v), (passages, pass_v), (pool, pool_v), (refs, refs_v),
            (count, count_v), (positive, pos_v), (queries, q_v)))
    ]
    for load in loads:
        load.start()

    loads[0].wait()
    eye = iota((slots, slots), 0) == iota((slots, slots), 1)
    pool_iota = iota((slots, pool_rows), 1).astype(jnp.float32)
    wanted = list_v[...].astype(jnp.float32)
    for o in range(owners):
        column = jnp.sum(jnp.where(eye, wanted[o:o + 1, :], 0.0), axis=1, keepdims=True)
        hot_out[o * slots:(o + 1) * slots, :] = (pool_iota == column).astype(jnp.float32).astype(jnp.bfloat16)

    def slot_rows(owner):
        return pl.ds(pl.multiple_of(owner * slots, slots), slots)

    def hot_copy(source, target, peer):
        return pltpu.make_async_remote_copy(
            src_ref=hot_out.at[slot_rows(target)], dst_ref=hot_in.at[slot_rows(source)],
            send_sem=hot_send.at[target], recv_sem=hot_recv.at[source],
            device_id={"grp": peer}, device_id_type=MESH)

    def row_copy(source, target, c, peer):
        return pltpu.make_async_remote_copy(
            src_ref=picked.at[c, slot_rows(target)], dst_ref=table.at[c, slot_rows(source)],
            send_sem=row_send.at[target, c], recv_sem=row_recv.at[source, c],
            device_id={"grp": peer}, device_id_type=MESH)

    def pass_copy(step):
        return pltpu.make_async_remote_copy(
            src_ref=packed.at[own_slot], dst_ref=packed.at[own_slot],
            send_sem=pass_send.at[step], recv_sem=pass_recv.at[step],
            device_id={"blk": lax.rem(blk + step, n_blk)}, device_id_type=MESH)

    @pl.when(jnp.logical_not(is_hub))
    def _():
        pl.semaphore_wait(barrier, owners - 1)
        for peer in peers:
            hot_copy(grp, peer, peer).start()

    @pl.when(is_hub)
    def _():
        for peer in peers:
            hot_copy(peer, grp, peer).wait_recv()
        for peer in peers:
            hot_copy(grp, peer, peer).start()

        def greet(step, carry):
            pl.semaphore_signal(
                barrier, inc=1, device_id={"blk": lax.rem(blk + step, n_blk)}, device_id_type=MESH)
            return carry

        lax.fori_loop(1, n_blk, greet, 0)

    loads[1].wait()
    own = pass_v[...].astype(jnp.float32)
    fold_iota = iota((TILE_ROWS, fold_w), 0)
    folded = jnp.zeros((TILE_ROWS, fold_w), jnp.float32)
    for c in range(folds):
        for j in range(p_dev):
            folded = jnp.where(fold_iota == c * p_dev + j, own[j:j + 1, c * fold_w:(c + 1) * fold_w], folded)
    own_slot = pl.ds(pl.multiple_of(blk * TILE_ROWS, TILE_ROWS), TILE_ROWS)
    packed[own_slot, :] = folded.astype(jnp.bfloat16)

    hot_in[slot_rows(grp), :] = hot_out[slot_rows(grp), :]

    def pick_rows(c, first, last):
        rows = dot_nn(hot_in[first * slots:last * slots, :], pool_v[:, c * width:(c + 1) * width])
        picked[c, first * slots:last * slots, :] = rows.astype(jnp.bfloat16)
        for peer in range(first, last):
            @pl.when(half != peer // 2)
            def _():
                row_copy(grp, peer, c, peer).start()

    def hot_arrived(peer):
        @pl.when(jnp.logical_and(jnp.logical_not(is_hub), grp != peer))
        def _():
            hot_copy(peer, grp, peer).wait_recv()

    loads[2].wait()
    for peer in range(1, owners):
        hot_arrived(peer)
    ahead = min(2, CHUNKS)

    def far_sent(c, first, last):
        for peer in range(first, last):
            @pl.when(half != peer // 2)
            def _():
                row_copy(grp, peer, c, peer).wait_send()

    def send_passes():
        def send(step, carry):
            pass_copy(step).start()
            return carry

        lax.fori_loop(1, n_blk, send, 0)

    for c in range(ahead):
        pick_rows(c, 1, owners)
    hot_arrived(0)
    for c in range(ahead):
        pick_rows(c, 0, 1)

    @pl.when(is_hub)
    def _():
        pl.semaphore_wait(barrier, n_blk - 1)
        for peer in peers:
            pl.semaphore_signal(go_sem, inc=1, device_id={"grp": peer}, device_id_type=MESH)

    @pl.when(jnp.logical_not(is_hub))
    def _():
        pl.semaphore_wait(go_sem, 1)

    send_passes()
    for c in range(ahead, CHUNKS):
        far_sent(c - ahead, 1, owners)
        pick_rows(c, 1, owners)
        far_sent(c - ahead, 0, 1)
        pick_rows(c, 0, 1)
    for c in range(CHUNKS):
        row_copy(grp, near, c, near).start()

    table[:, slot_rows(grp), :] = picked[:, slot_rows(grp), :]

    for load in loads[3:]:
        load.wait()
    hn = refs_v.shape[0]
    refs_t = jnp.where(iota((hn, q_rows), 0) < count_v[...], refs_v[...], -1)
    row_iota = iota((span, q_rows), 0)
    present = jnp.zeros((span, q_rows), jnp.float32)
    for i in range(hn):
        present = present + (row_iota == refs_t[i:i + 1, :]).astype(jnp.float32)

    def hard_part(c):
        cols = slice(c * width, (c + 1) * width)
        for peer in peers:
            row_copy(peer, grp, c, peer).wait_recv()
        return dot_nt(table[c, 0:span, :], q_v[:, cols])

    hard_logits = hard_part(0)
    for c in range(1, CHUNKS - 1):
        hard_logits = hard_logits + hard_part(c)

    def recv_pass(step, carry):
        pass_copy(step).wait()
        return carry

    lax.fori_loop(1, n_blk, recv_pass, 0)
    group_rows = folds * TILE_ROWS
    out_row, in_row = iota((group_rows, group_rows), 0), iota((group_rows, group_rows), 1)
    k = lax.rem(out_row, TILE_ROWS)
    source = lax.div(k, p_dev) * TILE_ROWS + lax.div(out_row, TILE_ROWS) * p_dev + lax.rem(k, p_dev)
    unfold = (source == in_row).astype(jnp.float32).astype(jnp.bfloat16)

    def unfold_group(i, carry):
        block = packed[pl.ds(pl.multiple_of(i * group_rows, group_rows), group_rows), :]
        rows = dot_nn(unfold, block).astype(jnp.bfloat16)
        place = pl.ds(pl.multiple_of(span + i * TILE_ROWS, TILE_ROWS), TILE_ROWS)
        for c in range(folds):
            at, within = divmod(c * fold_w, width)
            table[at, place, within:within + fold_w] = rows[c * TILE_ROWS:(c + 1) * TILE_ROWS, :]
        return carry

    lax.fori_loop(0, n_blk // folds, unfold_group, 0)
    cycle_logits = jnp.zeros((cycle, q_rows), jnp.float32)
    for c in range(CHUNKS):
        cols = slice(c * width, (c + 1) * width)
        cycle_logits = cycle_logits + dot_nt(table[c, span:span + cycle, :], q_v[:, cols])
    cycle_peak = jnp.max(cycle_logits, axis=0, keepdims=True)
    onehot = (iota((cycle, q_rows), 0) == pos_v[...]).astype(jnp.float32)
    chosen = jnp.sum(cycle_logits * onehot, axis=0, keepdims=True)

    hard_logits = hard_logits + hard_part(CHUNKS - 1)

    used = present > 0
    masked = jnp.where(used, hard_logits, -jnp.inf)
    peak = jnp.maximum(cycle_peak, jnp.max(masked, axis=0, keepdims=True))
    cycle_exp = jnp.exp(cycle_logits - peak)
    hard_exp = present * jnp.exp(jnp.where(used, hard_logits - peak, 0.0))
    denominator = jnp.sum(cycle_exp, axis=0, keepdims=True) + jnp.sum(hard_exp, axis=0, keepdims=True)
    loss[...] = jnp.log(denominator) + peak - chosen
    scale = 1.0 / denominator
    weights[:, 0:span] = (hard_exp * scale).T.astype(jnp.bfloat16)
    weights[:, span:span + cycle] = (cycle_exp * scale - onehot).T.astype(jnp.bfloat16)

    for peer in peers:
        hot_copy(grp, peer, peer).wait_send()
    for c in range(CHUNKS):
        row_copy(grp, near, c, near).wait_send()
    for c in range(CHUNKS - ahead, CHUNKS):
        far_sent(c, 0, owners)


def grad_kernel(table, weights, loss, grad, loss_out, grad_v, sems):
    tiles, _, width = table.shape
    copies = [pltpu.make_async_copy(loss, loss_out, sems.at[tiles])]
    copies[0].start()
    for c in range(tiles):
        cols = slice(c * width, (c + 1) * width)
        grad_v[:, cols] = dot_nn(weights[...], table[c]).astype(jnp.bfloat16)
        here = pl.ds(c * width, width)
        copies.append(pltpu.make_async_copy(grad_v.at[:, here], grad.at[:, here], sems.at[c]))
        copies[-1].start()
    for copy in copies:
        copy.wait()


def body(n_blk, queries, passages, pool, positive_ids, request_lists, hard_refs, hard_count):
    q_rows, depth = queries.shape
    p_dev = passages.shape[0]
    pool_rows = pool.shape[0]
    _, owners, slots = request_lists.shape
    hn = hard_refs.shape[1]
    span, cycle = owners * slots, n_blk * p_dev
    width = depth // CHUNKS
    bf16, f32, i32 = jnp.bfloat16, jnp.float32, jnp.int32
    dma = pltpu.SemaphoreType.DMA
    flops = 2 * depth * (2 * q_rows * (span + cycle) + span * pool_rows)
    in_vmem = pl.BlockSpec(memory_space=pltpu.VMEM)
    in_hbm = pl.BlockSpec(memory_space=pltpu.HBM)
    table, weights, loss = pl.pallas_call(
        functools.partial(kernel, n_blk),
        out_shape=(
            pltpu.VMEM((CHUNKS, span + cycle, width), bf16),
            pltpu.VMEM((q_rows, span + cycle), bf16),
            pltpu.VMEM((1, q_rows), f32),
        ),
        in_specs=[in_hbm] * 7,
        out_specs=(in_vmem,) * 3,
        scratch_shapes=[
            pltpu.VMEM((q_rows, depth), bf16),
            pltpu.VMEM((p_dev, depth), bf16),
            pltpu.VMEM((pool_rows, depth), bf16),
            pltpu.VMEM((1, q_rows), i32),
            pltpu.VMEM((owners, slots), i32),
            pltpu.VMEM((hn, q_rows), i32),
            pltpu.VMEM((1, q_rows), i32),
            pltpu.VMEM((span, pool_rows), bf16),
            pltpu.VMEM((span, pool_rows), bf16),
            pltpu.VMEM((CHUNKS, span, width), bf16),
            pltpu.VMEM((n_blk * TILE_ROWS, depth * p_dev // TILE_ROWS), bf16),
            dma((7,)), dma((owners,)), dma((owners,)), dma((owners, CHUNKS)), dma((owners, CHUNKS)),
            dma((n_blk,)), dma((n_blk,)), pltpu.SemaphoreType.REGULAR,
        ],
        compiler_params=pltpu.CompilerParams(
            collective_id=0, has_side_effects=True, vmem_limit_bytes=VMEM_LIMIT),
        cost_estimate=pl.CostEstimate(
            flops=flops, bytes_accessed=4 * q_rows * depth, transcendentals=q_rows * (span + cycle)),
    )(*(pltpu.with_memory_space_constraint(x, pltpu.HBM) for x in (
        queries, passages, pool, positive_ids.reshape(1, q_rows), request_lists.reshape(owners, slots),
        hard_refs.T, hard_count.reshape(1, q_rows))))
    grad, loss = pl.pallas_call(
        grad_kernel,
        out_shape=(pltpu.HBM((q_rows, depth), bf16), pltpu.HBM((1, q_rows), f32)),
        in_specs=[in_vmem] * 3,
        out_specs=(in_hbm,) * 2,
        scratch_shapes=[pltpu.VMEM((q_rows, depth), bf16), dma((CHUNKS + 1,))],
        compiler_params=pltpu.CompilerParams(vmem_limit_bytes=VMEM_LIMIT),
        cost_estimate=pl.CostEstimate(
            flops=2 * depth * q_rows * (span + cycle), bytes_accessed=2 * q_rows * depth, transcendentals=0),
    )(table, weights, loss)
    return grad, loss.reshape(q_rows)


def solution(mesh):
    rows = P(("blk", "grp"), None)
    return jax.shard_map(
        functools.partial(body, mesh.shape["blk"]),
        mesh=mesh,
        in_specs=(rows, rows, rows, P(("blk", "grp")), P(("blk", "grp"), None, None), rows, P(("blk", "grp"))),
        out_specs=(rows, P(("blk", "grp"))),
        check_vma=False,
    )
```

```python
import functools

import jax
import jax.numpy as jnp
from jax import lax
from jax.experimental import pallas as pl
from jax.experimental.pallas import tpu as pltpu
from jax.sharding import PartitionSpec as P

MESH = pl.DeviceIdType.MESH
VMEM_LIMIT = 32 * 2**20
TILE_ROWS = 16
TILES = 8
CHUNKS = ((0, 1), (1, 2), (3, 2), (5, 2), (7, 1))


def iota(shape, axis):
    return lax.broadcasted_iota(jnp.int32, shape, axis)


def dot_nt(a, b):
    return lax.dot_general(a, b, (((1,), (1,)), ((), ())), preferred_element_type=jnp.float32)


def dot_nn(a, b):
    return jnp.dot(a, b, preferred_element_type=jnp.float32)


def kernel(n_blk, queries, passages, pool, positive, lists, refs, count, table, weights, loss,
           q_v, pass_v, pool_v, pos_v, list_v, refs_v, count_v,
           hot_out, hot_in, picked, packed,
           load_sem, hot_send, hot_recv, row_send, row_recv, pass_send, pass_recv, go_sem):
    blk = lax.axis_index("blk")
    grp = lax.axis_index("grp")
    q_rows, depth = q_v.shape
    p_dev = pass_v.shape[0]
    pool_rows = pool_v.shape[0]
    owners, slots = list_v.shape
    span = owners * slots
    cycle = n_blk * p_dev
    folds = TILE_ROWS // p_dev
    fold_w = depth // folds
    width = depth // TILES

    half, core = lax.div(grp, 2), lax.rem(grp, 2)
    near, far_odd, far_even = half * 2 + 1 - core, (1 - half) * 2 + 1, (1 - half) * 2
    peers = (far_odd, far_even, near)
    is_hub = grp == 0

    barrier = pltpu.get_barrier_semaphore()
    for peer in peers:
        @pl.when(peer != 0)
        def _():
            pl.semaphore_signal(barrier, inc=1, device_id={"grp": peer}, device_id_type=MESH)

    loads = [
        pltpu.make_async_copy(src, dst, load_sem.at[i])
        for i, (src, dst) in enumerate((
            (lists, list_v), (passages, pass_v), (pool, pool_v), (refs, refs_v),
            (count, count_v), (positive, pos_v), (queries, q_v)))
    ]
    for load in loads:
        load.start()

    loads[0].wait()
    eye = iota((slots, slots), 0) == iota((slots, slots), 1)
    pool_iota = iota((slots, pool_rows), 1).astype(jnp.float32)
    wanted = list_v[...].astype(jnp.float32)
    for o in range(owners):
        column = jnp.sum(jnp.where(eye, wanted[o:o + 1, :], 0.0), axis=1, keepdims=True)
        hot_out[o * slots:(o + 1) * slots, :] = (pool_iota == column).astype(jnp.float32).astype(jnp.bfloat16)

    def slot_rows(owner):
        return pl.ds(pl.multiple_of(owner * slots, slots), slots)

    def hot_copy(source, target, peer):
        return pltpu.make_async_remote_copy(
            src_ref=hot_out.at[slot_rows(target)], dst_ref=hot_in.at[slot_rows(source)],
            send_sem=hot_send.at[target], recv_sem=hot_recv.at[source],
            device_id={"grp": peer}, device_id_type=MESH)

    def row_copy(source, target, c, peer):
        return pltpu.make_async_remote_copy(
            src_ref=picked.at[pl.ds(*CHUNKS[c]), slot_rows(target)],
            dst_ref=table.at[pl.ds(*CHUNKS[c]), slot_rows(source)],
            send_sem=row_send.at[target, c], recv_sem=row_recv.at[source, c],
            device_id={"grp": peer}, device_id_type=MESH)

    def pass_copy(step):
        return pltpu.make_async_remote_copy(
            src_ref=packed.at[own_slot], dst_ref=packed.at[own_slot],
            send_sem=pass_send.at[step], recv_sem=pass_recv.at[step],
            device_id={"blk": lax.rem(blk + step, n_blk)}, device_id_type=MESH)

    @pl.when(jnp.logical_not(is_hub))
    def _():
        pl.semaphore_wait(barrier, owners - 1)
        for peer in peers:
            hot_copy(grp, peer, peer).start()

    @pl.when(is_hub)
    def _():
        for peer in peers:
            hot_copy(peer, grp, peer).wait_recv()
        for peer in peers:
            hot_copy(grp, peer, peer).start()

        def greet(step, carry):
            pl.semaphore_signal(
                barrier, inc=1, device_id={"blk": lax.rem(blk + step, n_blk)}, device_id_type=MESH)
            return carry

        lax.fori_loop(1, n_blk, greet, 0)

    loads[1].wait()
    own = pass_v[...].astype(jnp.float32)
    fold_iota = iota((TILE_ROWS, fold_w), 0)
    folded = jnp.zeros((TILE_ROWS, fold_w), jnp.float32)
    for c in range(folds):
        for j in range(p_dev):
            folded = jnp.where(fold_iota == c * p_dev + j, own[j:j + 1, c * fold_w:(c + 1) * fold_w], folded)
    own_slot = pl.ds(pl.multiple_of(blk * TILE_ROWS, TILE_ROWS), TILE_ROWS)
    packed[own_slot, :] = folded.astype(jnp.bfloat16)

    hot_in[slot_rows(grp), :] = hot_out[slot_rows(grp), :]

    def pick_rows(c, first, last):
        tile, count = CHUNKS[c]
        cols = slice(tile * width, (tile + count) * width)
        rows = dot_nn(hot_in[first * slots:last * slots, :], pool_v[:, cols]).astype(jnp.bfloat16)
        for t in range(count):
            picked[tile + t, first * slots:last * slots, :] = rows[:, t * width:(t + 1) * width]
        for peer in range(first, last):
            @pl.when(half != peer // 2)
            def _():
                row_copy(grp, peer, c, peer).start()

    def hot_arrived(peer):
        @pl.when(jnp.logical_and(jnp.logical_not(is_hub), grp != peer))
        def _():
            hot_copy(peer, grp, peer).wait_recv()

    loads[2].wait()
    for peer in range(1, owners):
        hot_arrived(peer)
    for c in range(len(CHUNKS)):
        pick_rows(c, 1, owners)
    hot_arrived(0)
    for c in range(len(CHUNKS)):
        pick_rows(c, 0, 1)
    for c in range(len(CHUNKS)):
        row_copy(grp, near, c, near).start()

    @pl.when(is_hub)
    def _():
        pl.semaphore_wait(barrier, n_blk - 1)
        for peer in peers:
            pl.semaphore_signal(go_sem, inc=1, device_id={"grp": peer}, device_id_type=MESH)

    @pl.when(jnp.logical_not(is_hub))
    def _():
        pl.semaphore_wait(go_sem, 1)

    def send_pass(step, carry):
        pass_copy(step).start()
        return carry

    lax.fori_loop(1, n_blk, send_pass, 0)

    table[:, slot_rows(grp), :] = picked[:, slot_rows(grp), :]

    for load in loads[3:]:
        load.wait()
    hn = refs_v.shape[0]
    refs_t = jnp.where(iota((hn, q_rows), 0) < count_v[...], refs_v[...], -1)
    row_iota = iota((span, q_rows), 0)
    present = jnp.zeros((span, q_rows), jnp.float32)
    for i in range(hn):
        present = present + (row_iota == refs_t[i:i + 1, :]).astype(jnp.float32)

    def hard_part(c):
        for peer in peers:
            row_copy(peer, grp, c, peer).wait_recv()
        tile, count = CHUNKS[c]
        return sum(
            dot_nt(table[t, 0:span, :], q_v[:, t * width:(t + 1) * width])
            for t in range(tile, tile + count))

    hard_logits = hard_part(0)
    for c in range(1, len(CHUNKS) - 1):
        hard_logits = hard_logits + hard_part(c)

    def recv_pass(step, carry):
        pass_copy(step).wait()
        return carry

    lax.fori_loop(1, n_blk, recv_pass, 0)
    group_rows = folds * TILE_ROWS
    out_row, in_row = iota((group_rows, group_rows), 0), iota((group_rows, group_rows), 1)
    k = lax.rem(out_row, TILE_ROWS)
    source = lax.div(k, p_dev) * TILE_ROWS + lax.div(out_row, TILE_ROWS) * p_dev + lax.rem(k, p_dev)
    unfold = (source == in_row).astype(jnp.float32).astype(jnp.bfloat16)

    def unfold_group(i, carry):
        block = packed[pl.ds(pl.multiple_of(i * group_rows, group_rows), group_rows), :]
        rows = dot_nn(unfold, block).astype(jnp.bfloat16)
        place = pl.ds(pl.multiple_of(span + i * TILE_ROWS, TILE_ROWS), TILE_ROWS)
        for c in range(folds):
            at, within = divmod(c * fold_w, width)
            table[at, place, within:within + fold_w] = rows[c * TILE_ROWS:(c + 1) * TILE_ROWS, :]
        return carry

    lax.fori_loop(0, n_blk // folds, unfold_group, 0)
    cycle_logits = jnp.zeros((cycle, q_rows), jnp.float32)
    for c in range(TILES):
        cols = slice(c * width, (c + 1) * width)
        cycle_logits = cycle_logits + dot_nt(table[c, span:span + cycle, :], q_v[:, cols])
    cycle_peak = jnp.max(cycle_logits, axis=0, keepdims=True)
    onehot = (iota((cycle, q_rows), 0) == pos_v[...]).astype(jnp.float32)
    chosen = jnp.sum(cycle_logits * onehot, axis=0, keepdims=True)

    hard_logits = hard_logits + hard_part(len(CHUNKS) - 1)

    used = present > 0
    masked = jnp.where(used, hard_logits, -jnp.inf)
    peak = jnp.maximum(cycle_peak, jnp.max(masked, axis=0, keepdims=True))
    cycle_exp = jnp.exp(cycle_logits - peak)
    hard_exp = present * jnp.exp(jnp.where(used, hard_logits - peak, 0.0))
    denominator = jnp.sum(cycle_exp, axis=0, keepdims=True) + jnp.sum(hard_exp, axis=0, keepdims=True)
    loss[...] = jnp.log(denominator) + peak - chosen
    scale = 1.0 / denominator
    weights[:, 0:span] = (hard_exp * scale).T.astype(jnp.bfloat16)
    weights[:, span:span + cycle] = (cycle_exp * scale - onehot).T.astype(jnp.bfloat16)

    for peer in peers:
        hot_copy(grp, peer, peer).wait_send()
        for c in range(len(CHUNKS)):
            row_copy(grp, peer, c, peer).wait_send()


def grad_kernel(table, weights, loss, grad, loss_out, grad_v, sems):
    tiles, _, width = table.shape
    copies = [pltpu.make_async_copy(loss, loss_out, sems.at[tiles])]
    copies[0].start()
    for c in range(tiles):
        cols = slice(c * width, (c + 1) * width)
        grad_v[:, cols] = dot_nn(weights[...], table[c]).astype(jnp.bfloat16)
        here = pl.ds(c * width, width)
        copies.append(pltpu.make_async_copy(grad_v.at[:, here], grad.at[:, here], sems.at[c]))
        copies[-1].start()
    for copy in copies:
        copy.wait()


def body(n_blk, queries, passages, pool, positive_ids, request_lists, hard_refs, hard_count):
    q_rows, depth = queries.shape
    p_dev = passages.shape[0]
    pool_rows = pool.shape[0]
    _, owners, slots = request_lists.shape
    hn = hard_refs.shape[1]
    span, cycle = owners * slots, n_blk * p_dev
    width = depth // TILES
    bf16, f32, i32 = jnp.bfloat16, jnp.float32, jnp.int32
    dma = pltpu.SemaphoreType.DMA
    flops = 2 * depth * (2 * q_rows * (span + cycle) + span * pool_rows)
    in_vmem = pl.BlockSpec(memory_space=pltpu.VMEM)
    in_hbm = pl.BlockSpec(memory_space=pltpu.HBM)
    table, weights, loss = pl.pallas_call(
        functools.partial(kernel, n_blk),
        out_shape=(
            pltpu.VMEM((TILES, span + cycle, width), bf16),
            pltpu.VMEM((q_rows, span + cycle), bf16),
            pltpu.VMEM((1, q_rows), f32),
        ),
        in_specs=[in_hbm] * 7,
        out_specs=(in_vmem,) * 3,
        scratch_shapes=[
            pltpu.VMEM((q_rows, depth), bf16),
            pltpu.VMEM((p_dev, depth), bf16),
            pltpu.VMEM((pool_rows, depth), bf16),
            pltpu.VMEM((1, q_rows), i32),
            pltpu.VMEM((owners, slots), i32),
            pltpu.VMEM((hn, q_rows), i32),
            pltpu.VMEM((1, q_rows), i32),
            pltpu.VMEM((span, pool_rows), bf16),
            pltpu.VMEM((span, pool_rows), bf16),
            pltpu.VMEM((TILES, span, width), bf16),
            pltpu.VMEM((n_blk * TILE_ROWS, depth * p_dev // TILE_ROWS), bf16),
            dma((7,)), dma((owners,)), dma((owners,)), dma((owners, len(CHUNKS))), dma((owners, len(CHUNKS))),
            dma((n_blk,)), dma((n_blk,)), pltpu.SemaphoreType.REGULAR,
        ],
        compiler_params=pltpu.CompilerParams(
            collective_id=0, has_side_effects=True, vmem_limit_bytes=VMEM_LIMIT),
        cost_estimate=pl.CostEstimate(
            flops=flops, bytes_accessed=4 * q_rows * depth, transcendentals=q_rows * (span + cycle)),
    )(*(pltpu.with_memory_space_constraint(x, pltpu.HBM) for x in (
        queries, passages, pool, positive_ids.reshape(1, q_rows), request_lists.reshape(owners, slots),
        hard_refs.T, hard_count.reshape(1, q_rows))))
    grad, loss = pl.pallas_call(
        grad_kernel,
        out_shape=(pltpu.HBM((q_rows, depth), bf16), pltpu.HBM((1, q_rows), f32)),
        in_specs=[in_vmem] * 3,
        out_specs=(in_hbm,) * 2,
        scratch_shapes=[pltpu.VMEM((q_rows, depth), bf16), dma((TILES + 1,))],
        compiler_params=pltpu.CompilerParams(vmem_limit_bytes=VMEM_LIMIT),
        cost_estimate=pl.CostEstimate(
            flops=2 * depth * q_rows * (span + cycle), bytes_accessed=2 * q_rows * depth, transcendentals=0),
    )(table, weights, loss)
    return grad, loss.reshape(q_rows)


def solution(mesh):
    rows = P(("blk", "grp"), None)
    return jax.shard_map(
        functools.partial(body, mesh.shape["blk"]),
        mesh=mesh,
        in_specs=(rows, rows, rows, P(("blk", "grp")), P(("blk", "grp"), None, None), rows, P(("blk", "grp"))),
        out_specs=(rows, P(("blk", "grp"))),
        check_vma=False,
    )
```

```python
import functools

import jax
import jax.numpy as jnp
from jax import lax
from jax.experimental import pallas as pl
from jax.experimental.pallas import tpu as pltpu
from jax.sharding import PartitionSpec as P

MESH = pl.DeviceIdType.MESH
VMEM_LIMIT = 32 * 2**20
TILE_ROWS = 16
TILES = 4
CHUNKS = ((0, 1), (1, 2), (3, 1))


def iota(shape, axis):
    return lax.broadcasted_iota(jnp.int32, shape, axis)


def dot_nt(a, b):
    return lax.dot_general(a, b, (((1,), (1,)), ((), ())), preferred_element_type=jnp.float32)


def dot_nn(a, b):
    return jnp.dot(a, b, preferred_element_type=jnp.float32)


def kernel(n_blk, queries, passages, pool, positive, lists, refs, count, table, weights, loss,
           q_v, pass_v, pool_v, pos_v, list_v, refs_v, count_v,
           hot_out, hot_in, picked, packed,
           load_sem, hot_send, hot_recv, row_send, row_recv, pass_send, pass_recv, go_sem):
    blk = lax.axis_index("blk")
    grp = lax.axis_index("grp")
    q_rows, depth = q_v.shape
    p_dev = pass_v.shape[0]
    pool_rows = pool_v.shape[0]
    owners, slots = list_v.shape
    span = owners * slots
    cycle = n_blk * p_dev
    folds = TILE_ROWS // p_dev
    fold_w = depth // folds
    width = depth // TILES

    half, core = lax.div(grp, 2), lax.rem(grp, 2)
    near, far_odd, far_even = half * 2 + 1 - core, (1 - half) * 2 + 1, (1 - half) * 2
    peers = (far_odd, far_even, near)
    is_hub = grp == 0

    barrier = pltpu.get_barrier_semaphore()
    for peer in peers:
        @pl.when(peer != 0)
        def _():
            pl.semaphore_signal(barrier, inc=1, device_id={"grp": peer}, device_id_type=MESH)

    loads = [
        pltpu.make_async_copy(src, dst, load_sem.at[i])
        for i, (src, dst) in enumerate((
            (lists, list_v), (passages, pass_v), (pool, pool_v), (refs, refs_v),
            (count, count_v), (positive, pos_v), (queries, q_v)))
    ]
    for load in loads:
        load.start()

    loads[0].wait()
    eye = iota((slots, slots), 0) == iota((slots, slots), 1)
    pool_iota = iota((slots, pool_rows), 1).astype(jnp.float32)
    wanted = list_v[...].astype(jnp.float32)
    for o in range(owners):
        column = jnp.sum(jnp.where(eye, wanted[o:o + 1, :], 0.0), axis=1, keepdims=True)
        hot_out[o * slots:(o + 1) * slots, :] = (pool_iota == column).astype(jnp.float32).astype(jnp.bfloat16)

    def slot_rows(owner):
        return pl.ds(pl.multiple_of(owner * slots, slots), slots)

    def hot_copy(source, target, peer):
        return pltpu.make_async_remote_copy(
            src_ref=hot_out.at[slot_rows(target)], dst_ref=hot_in.at[slot_rows(source)],
            send_sem=hot_send.at[target], recv_sem=hot_recv.at[source],
            device_id={"grp": peer}, device_id_type=MESH)

    def row_copy(source, target, c, peer):
        return pltpu.make_async_remote_copy(
            src_ref=picked.at[pl.ds(*CHUNKS[c]), slot_rows(target)],
            dst_ref=table.at[pl.ds(*CHUNKS[c]), slot_rows(source)],
            send_sem=row_send.at[target, c], recv_sem=row_recv.at[source, c],
            device_id={"grp": peer}, device_id_type=MESH)

    def pass_copy(step):
        return pltpu.make_async_remote_copy(
            src_ref=packed.at[own_slot], dst_ref=packed.at[own_slot],
            send_sem=pass_send.at[step], recv_sem=pass_recv.at[step],
            device_id={"blk": lax.rem(blk + step, n_blk)}, device_id_type=MESH)

    @pl.when(jnp.logical_not(is_hub))
    def _():
        pl.semaphore_wait(barrier, owners - 1)
        for peer in peers:
            hot_copy(grp, peer, peer).start()

    @pl.when(is_hub)
    def _():
        for peer in peers:
            hot_copy(peer, grp, peer).wait_recv()
        for peer in peers:
            hot_copy(grp, peer, peer).start()

        def greet(step, carry):
            pl.semaphore_signal(
                barrier, inc=1, device_id={"blk": lax.rem(blk + step, n_blk)}, device_id_type=MESH)
            return carry

        lax.fori_loop(1, n_blk, greet, 0)

    loads[1].wait()
    own = pass_v[...].astype(jnp.float32)
    fold_iota = iota((TILE_ROWS, fold_w), 0)
    folded = jnp.zeros((TILE_ROWS, fold_w), jnp.float32)
    for c in range(folds):
        for j in range(p_dev):
            folded = jnp.where(fold_iota == c * p_dev + j, own[j:j + 1, c * fold_w:(c + 1) * fold_w], folded)
    own_slot = pl.ds(pl.multiple_of(blk * TILE_ROWS, TILE_ROWS), TILE_ROWS)
    packed[own_slot, :] = folded.astype(jnp.bfloat16)

    hot_in[slot_rows(grp), :] = hot_out[slot_rows(grp), :]

    def pick_rows(c, first, last):
        tile, count = CHUNKS[c]
        cols = slice(tile * width, (tile + count) * width)
        rows = dot_nn(hot_in[first * slots:last * slots, :], pool_v[:, cols]).astype(jnp.bfloat16)
        for t in range(count):
            picked[tile + t, first * slots:last * slots, :] = rows[:, t * width:(t + 1) * width]
        for peer in range(first, last):
            @pl.when(half != peer // 2)
            def _():
                row_copy(grp, peer, c, peer).start()

    def hot_arrived(peer):
        @pl.when(jnp.logical_and(jnp.logical_not(is_hub), grp != peer))
        def _():
            hot_copy(peer, grp, peer).wait_recv()

    loads[2].wait()
    for peer in range(1, owners):
        hot_arrived(peer)
    for c in range(len(CHUNKS)):
        pick_rows(c, 1, owners)
    hot_arrived(0)
    for c in range(len(CHUNKS)):
        pick_rows(c, 0, 1)
    for c in range(len(CHUNKS)):
        row_copy(grp, near, c, near).start()

    @pl.when(is_hub)
    def _():
        pl.semaphore_wait(barrier, n_blk - 1)
        for peer in peers:
            pl.semaphore_signal(go_sem, inc=1, device_id={"grp": peer}, device_id_type=MESH)

    @pl.when(jnp.logical_not(is_hub))
    def _():
        pl.semaphore_wait(go_sem, 1)

    def send_pass(step, carry):
        pass_copy(step).start()
        return carry

    lax.fori_loop(1, n_blk, send_pass, 0)

    table[:, slot_rows(grp), :] = picked[:, slot_rows(grp), :]

    for load in loads[3:]:
        load.wait()
    hn = refs_v.shape[0]
    refs_t = jnp.where(iota((hn, q_rows), 0) < count_v[...], refs_v[...], -1)
    row_iota = iota((span, q_rows), 0)
    present = jnp.zeros((span, q_rows), jnp.float32)
    for i in range(hn):
        present = present + (row_iota == refs_t[i:i + 1, :]).astype(jnp.float32)

    def hard_part(c):
        for peer in peers:
            row_copy(peer, grp, c, peer).wait_recv()
        tile, count = CHUNKS[c]
        return sum(
            dot_nt(table[t, 0:span, :], q_v[:, t * width:(t + 1) * width])
            for t in range(tile, tile + count))

    hard_logits = hard_part(0)
    for c in range(1, len(CHUNKS) - 1):
        hard_logits = hard_logits + hard_part(c)

    def recv_pass(step, carry):
        pass_copy(step).wait()
        return carry

    lax.fori_loop(1, n_blk, recv_pass, 0)
    group_rows = folds * TILE_ROWS
    out_row, in_row = iota((group_rows, group_rows), 0), iota((group_rows, group_rows), 1)
    k = lax.rem(out_row, TILE_ROWS)
    source = lax.div(k, p_dev) * TILE_ROWS + lax.div(out_row, TILE_ROWS) * p_dev + lax.rem(k, p_dev)
    unfold = (source == in_row).astype(jnp.float32).astype(jnp.bfloat16)

    def unfold_group(i, carry):
        block = packed[pl.ds(pl.multiple_of(i * group_rows, group_rows), group_rows), :]
        rows = dot_nn(unfold, block).astype(jnp.bfloat16)
        place = pl.ds(pl.multiple_of(span + i * TILE_ROWS, TILE_ROWS), TILE_ROWS)
        for c in range(folds):
            at, within = divmod(c * fold_w, width)
            table[at, place, within:within + fold_w] = rows[c * TILE_ROWS:(c + 1) * TILE_ROWS, :]
        return carry

    lax.fori_loop(0, n_blk // folds, unfold_group, 0)
    cycle_logits = jnp.zeros((cycle, q_rows), jnp.float32)
    for c in range(TILES):
        cols = slice(c * width, (c + 1) * width)
        cycle_logits = cycle_logits + dot_nt(table[c, span:span + cycle, :], q_v[:, cols])
    cycle_peak = jnp.max(cycle_logits, axis=0, keepdims=True)
    onehot = (iota((cycle, q_rows), 0) == pos_v[...]).astype(jnp.float32)
    chosen = jnp.sum(cycle_logits * onehot, axis=0, keepdims=True)

    hard_logits = hard_logits + hard_part(len(CHUNKS) - 1)

    used = present > 0
    masked = jnp.where(used, hard_logits, -jnp.inf)
    peak = jnp.maximum(cycle_peak, jnp.max(masked, axis=0, keepdims=True))
    cycle_exp = jnp.exp(cycle_logits - peak)
    hard_exp = present * jnp.exp(jnp.where(used, hard_logits - peak, 0.0))
    denominator = jnp.sum(cycle_exp, axis=0, keepdims=True) + jnp.sum(hard_exp, axis=0, keepdims=True)
    loss[...] = jnp.log(denominator) + peak - chosen
    scale = 1.0 / denominator
    weights[:, 0:span] = (hard_exp * scale).T.astype(jnp.bfloat16)
    weights[:, span:span + cycle] = (cycle_exp * scale - onehot).T.astype(jnp.bfloat16)

    for peer in peers:
        hot_copy(grp, peer, peer).wait_send()
        for c in range(len(CHUNKS)):
            row_copy(grp, peer, c, peer).wait_send()


def grad_kernel(table, weights, loss, grad, loss_out, grad_v, sems):
    tiles, _, width = table.shape
    copies = [pltpu.make_async_copy(loss, loss_out, sems.at[tiles])]
    copies[0].start()
    for c in range(tiles):
        cols = slice(c * width, (c + 1) * width)
        grad_v[:, cols] = dot_nn(weights[...], table[c]).astype(jnp.bfloat16)
        here = pl.ds(c * width, width)
        copies.append(pltpu.make_async_copy(grad_v.at[:, here], grad.at[:, here], sems.at[c]))
        copies[-1].start()
    for copy in copies:
        copy.wait()


def body(n_blk, queries, passages, pool, positive_ids, request_lists, hard_refs, hard_count):
    q_rows, depth = queries.shape
    p_dev = passages.shape[0]
    pool_rows = pool.shape[0]
    _, owners, slots = request_lists.shape
    hn = hard_refs.shape[1]
    span, cycle = owners * slots, n_blk * p_dev
    width = depth // TILES
    bf16, f32, i32 = jnp.bfloat16, jnp.float32, jnp.int32
    dma = pltpu.SemaphoreType.DMA
    flops = 2 * depth * (2 * q_rows * (span + cycle) + span * pool_rows)
    in_vmem = pl.BlockSpec(memory_space=pltpu.VMEM)
    in_hbm = pl.BlockSpec(memory_space=pltpu.HBM)
    table, weights, loss = pl.pallas_call(
        functools.partial(kernel, n_blk),
        out_shape=(
            pltpu.VMEM((TILES, span + cycle, width), bf16),
            pltpu.VMEM((q_rows, span + cycle), bf16),
            pltpu.VMEM((1, q_rows), f32),
        ),
        in_specs=[in_hbm] * 7,
        out_specs=(in_vmem,) * 3,
        scratch_shapes=[
            pltpu.VMEM((q_rows, depth), bf16),
            pltpu.VMEM((p_dev, depth), bf16),
            pltpu.VMEM((pool_rows, depth), bf16),
            pltpu.VMEM((1, q_rows), i32),
            pltpu.VMEM((owners, slots), i32),
            pltpu.VMEM((hn, q_rows), i32),
            pltpu.VMEM((1, q_rows), i32),
            pltpu.VMEM((span, pool_rows), bf16),
            pltpu.VMEM((span, pool_rows), bf16),
            pltpu.VMEM((TILES, span, width), bf16),
            pltpu.VMEM((n_blk * TILE_ROWS, depth * p_dev // TILE_ROWS), bf16),
            dma((7,)), dma((owners,)), dma((owners,)), dma((owners, len(CHUNKS))), dma((owners, len(CHUNKS))),
            dma((n_blk,)), dma((n_blk,)), pltpu.SemaphoreType.REGULAR,
        ],
        compiler_params=pltpu.CompilerParams(
            collective_id=0, has_side_effects=True, vmem_limit_bytes=VMEM_LIMIT),
        cost_estimate=pl.CostEstimate(
            flops=flops, bytes_accessed=4 * q_rows * depth, transcendentals=q_rows * (span + cycle)),
    )(*(pltpu.with_memory_space_constraint(x, pltpu.HBM) for x in (
        queries, passages, pool, positive_ids.reshape(1, q_rows), request_lists.reshape(owners, slots),
        hard_refs.T, hard_count.reshape(1, q_rows))))
    grad, loss = pl.pallas_call(
        grad_kernel,
        out_shape=(pltpu.HBM((q_rows, depth), bf16), pltpu.HBM((1, q_rows), f32)),
        in_specs=[in_vmem] * 3,
        out_specs=(in_hbm,) * 2,
        scratch_shapes=[pltpu.VMEM((q_rows, depth), bf16), dma((TILES + 1,))],
        compiler_params=pltpu.CompilerParams(vmem_limit_bytes=VMEM_LIMIT),
        cost_estimate=pl.CostEstimate(
            flops=2 * depth * q_rows * (span + cycle), bytes_accessed=2 * q_rows * depth, transcendentals=0),
    )(table, weights, loss)
    return grad, loss.reshape(q_rows)


def solution(mesh):
    rows = P(("blk", "grp"), None)
    return jax.shard_map(
        functools.partial(body, mesh.shape["blk"]),
        mesh=mesh,
        in_specs=(rows, rows, rows, P(("blk", "grp")), P(("blk", "grp"), None, None), rows, P(("blk", "grp"))),
        out_specs=(rows, P(("blk", "grp"))),
        check_vma=False,
    )
```
